512 devices in a mesh: samp: 16 (over z, x_hi), par: 32 (over x_lo, y, core).
Axes of the slice: x: 4 (x_hi: 2, x_lo: 2; x = x_hi * 2 + x_lo), y: 8, z: 8, core: 2. Of those that a mesh axis runs over, the one named last changes fastest.
Arguments:
- samples: bfloat16 [2048, 262144], P('samp', 'par'), may hold values from -1 to 1
- shift: float32 [2048], P('samp'), may hold values from 0.1 to 1
- panel_ids: int32 [16], replicated, may hold values from 0 to 15, each once
Outputs:
- factor_columns: float32 [2048, 256], P('samp')
The draws below stay inside these ranges and needn't reach their ends.
Inputs may be any that keep to these rules, and one draw needn't show every extreme that they name: `panel_ids`: each block number once.
All inputs are finite; a program needn't handle non-finite values.
Results may differ from the reference program's by a relative error of at most 0.0003.
Values may be sent and summed in bfloat16 or wider, within the bound.
No kernel may reach another device: no remote copies, remote signals or barrier semaphores. Data moves between devices by JAX's collectives and lax.ppermute only.
A program may use at most 64 MiB of HBM per device.

```python
import math
import jax
import jax.numpy as jnp
from jax import lax

P_SIZE = 262144
S_DEV = 128
N_S = 2048
N_SAMP = 16


def draw_samples(key, part):
    key_cluster, key_common, key_noise = jax.random.split(key, 3)
    clusters = max(N_S // 16, 1)
    member = jax.random.randint(key_cluster, (N_S,), 0, clusters)
    common = jax.random.normal(key_common, (clusters, P_SIZE), jnp.float32)
    noise = jax.random.normal(key_noise, (N_S, P_SIZE), jnp.float32)
    column = 3.0 ** (jnp.arange(P_SIZE, dtype=jnp.float32) / P_SIZE)
    mixed = (noise + common[member]) / math.sqrt(2.0)
    return (mixed * column[None, :] / math.sqrt(P_SIZE * 8.0 / math.log(9.0))).astype(jnp.bfloat16)


def block_levels(key, dims, pieces, least, largest):
    def one(axis_at, blocks):
        heights = jax.random.uniform(jax.random.fold_in(jax.random.fold_in(key, 6), axis_at), (blocks,), jnp.float32, least / len(pieces), largest / len(pieces))
        return jnp.repeat(jnp.exp(heights), dims[axis_at] // blocks).reshape((-1,) + (1,) * (len(dims) - axis_at - 1))

    level = one(*pieces[0])
    for cut in pieces[1:]:
        level = level * one(*cut)
    return level


def setup_inputs(seed: int = 0) -> dict:
    key_of = jax.random.split(jax.random.key(seed), 4)
    samples = draw_samples(jax.random.fold_in(key_of[3], 71), 0)
    shift = jnp.clip(jnp.exp(math.log(1.0) - 2.3025851 * jax.random.uniform(key_of[1], (N_S,), jnp.float32) ** block_levels(key_of[1], (N_S,), ((0, 16),), -0.2, 0.2)), 0.1, 1.0)
    panel_ids = jax.random.permutation(key_of[2], N_SAMP).astype(jnp.int32)
    return dict(samples=samples, shift=shift, panel_ids=panel_ids)


def solve_rows(block, matrix):
    factor = jnp.linalg.cholesky(block)
    return jax.scipy.linalg.solve_triangular(factor, matrix.T, lower=True).T

def shift_term(shift, owner):
    index = jnp.arange(N_S, dtype=jnp.int32)
    block_of = index // S_DEV
    within = index % S_DEV
    target = jnp.arange(S_DEV, dtype=jnp.int32)
    hit = (block_of == owner)[:, None] & (within[:, None] == target[None, :])
    return jnp.where(hit, shift[:, None], jnp.zeros((N_S, S_DEV), jnp.float32))

def block_rows(matrix, owner):
    return lax.dynamic_slice_in_dim(matrix, (owner * S_DEV).astype(jnp.int32), S_DEV, 0)

def reference(samples, shift, panel_ids):
    first_owner = panel_ids[0]
    second_owner = panel_ids[1]
    panel_zero = block_rows(samples, first_owner)
    panel_one = block_rows(samples, second_owner)
    gram_zero = jnp.dot(samples.astype(jnp.float32), panel_zero.T.astype(jnp.float32), preferred_element_type=jnp.float32)
    gram_one = jnp.dot(samples.astype(jnp.float32), panel_one.T.astype(jnp.float32), preferred_element_type=jnp.float32)
    shifted_zero = gram_zero + shift_term(shift, first_owner)
    column_zero = solve_rows(block_rows(shifted_zero, first_owner), shifted_zero)
    remote_rows = block_rows(column_zero, second_owner)
    update = jnp.dot(column_zero.astype(jnp.float32), remote_rows.T.astype(jnp.float32), precision=lax.Precision.HIGHEST, preferred_element_type=jnp.float32)
    shifted_one = gram_one + shift_term(shift, second_owner) - update
    column_one = solve_rows(block_rows(shifted_one, second_owner), shifted_one)
    return jnp.concatenate([column_zero, column_one], axis=1)
```

```python
import jax
import jax.numpy as jnp
from jax import lax
from jax.sharding import PartitionSpec as P

ROWS = 128
SAMP = 16
PAR = 32
CHIPS = PAR // 2
STRIP = ROWS // CHIPS
HIGHEST = lax.Precision.HIGHEST


def swap_cores(block):
    return lax.ppermute(block, "par", [(i, i ^ 1) for i in range(PAR)])


def rows_times(left, right):
    return lax.dot_general(
        left, right, (((1,), (1,)), ((), ())), preferred_element_type=jnp.float32
    )


def exact_rows_times(left, right):
    return lax.dot_general(
        left, right, (((1,), (1,)), ((), ())),
        precision=HIGHEST, preferred_element_type=jnp.float32,
    )


def solve_rows(block, matrix):
    factor = jnp.linalg.cholesky(block)
    return jax.scipy.linalg.solve_triangular(factor, matrix.T, lower=True).T


def per_device(samples, shift, panel_ids):
    width = samples.shape[1] // SAMP
    here = lax.axis_index("samp")
    place = lax.axis_index("par")
    core = place % 2
    chip = place // 2

    pieces = samples.reshape(ROWS, SAMP, width).transpose(1, 0, 2)
    pieces = lax.all_to_all(pieces, "samp", 0, 0, tiled=True)
    every = pieces.reshape(SAMP * ROWS, width)

    def partial(k):
        panel = lax.dynamic_index_in_dim(pieces, panel_ids[k], 0, keepdims=False)
        return rows_times(every, panel)

    total = partial(core) + swap_cores(partial(1 - core))

    strips = total.reshape(SAMP, CHIPS, STRIP, ROWS).transpose(1, 0, 2, 3)
    groups = [[2 * i + c for i in range(CHIPS)] for c in range(2)]
    strips = lax.all_to_all(strips, "par", 0, 0, axis_index_groups=groups, tiled=True)
    strips = strips.sum(0)

    row = chip * STRIP + jnp.arange(STRIP)
    mine = lax.dynamic_slice_in_dim(shift, chip * STRIP, STRIP, 0)
    owner = panel_ids[core] == here
    extra = jnp.where(
        (row[:, None] == jnp.arange(ROWS)[None, :]) & owner, mine[:, None], 0.0
    )
    strips = jnp.where(
        (jnp.arange(SAMP) == here)[:, None, None], strips + extra[None], strips
    )

    def rows_of(k):
        return jnp.broadcast_to(
            lax.dynamic_index_in_dim(strips, panel_ids[k], 0, keepdims=False)[None],
            strips.shape,
        )

    three = jnp.stack([strips, rows_of(0), rows_of(1)], 1)
    three = lax.all_to_all(three, "samp", 0, 0, tiled=True).sum(0)

    copies = jnp.broadcast_to(three[None], (PAR,) + three.shape)
    gathered = lax.all_to_all(copies, "par", 0, 0, tiled=True)
    gathered = gathered.reshape(CHIPS, 2, 3, STRIP, ROWS).transpose(2, 1, 0, 3, 4)
    gathered = gathered.reshape(3, 2, ROWS, ROWS)
    own, first, second = gathered[0], gathered[1], gathered[2]

    both = jnp.concatenate([own[0], second[0]], 0)
    solved = solve_rows(first[0], both)
    column_zero, remote = solved[:ROWS], solved[ROWS:]
    both = jnp.concatenate([own[1], second[1]], 0) - exact_rows_times(solved, remote)
    column_one = solve_rows(both[ROWS:], both[:ROWS])
    return jnp.concatenate([column_zero, column_one], axis=1)


def solution(mesh):
    placed = (P("samp", "par"), P("samp"), P())
    return jax.shard_map(
        per_device, mesh=mesh, in_specs=placed, out_specs=P("samp", None), check_vma=False
    )
```

```python
import jax
import jax.numpy as jnp
from jax import lax
from jax.experimental import pallas as pl
from jax.experimental.pallas import tpu as pltpu
from jax.sharding import PartitionSpec as P

ROWS = 128
SAMP = 16
PAR = 32
CHIPS = PAR // 2
TILE = 8
TILES = ROWS // TILE
HIGHEST = lax.Precision.HIGHEST

CHIPS_BY_CORE = [[2 * x + c for x in range(CHIPS)] for c in range(2)]


def exact(left, right, contract):
    return lax.dot_general(
        left, right, (contract, ((), ())),
        precision=HIGHEST, preferred_element_type=jnp.float32,
    )


def inverse_factor(matrix):
    lane = lax.broadcasted_iota(jnp.int32, (TILE, ROWS), 1)
    sub = lax.broadcasted_iota(jnp.int32, (TILE, ROWS), 0)
    lanes = lane[:1]
    tiles = [matrix[t * TILE:(t + 1) * TILE] for t in range(TILES)]
    for at in range(TILES):
        base = at * TILE
        rows = [tiles[at][r:r + 1] for r in range(TILE)]
        pivot = [
            [jnp.broadcast_to(rows[r][:, base + c:base + c + 1], (1, ROWS)) if c >= r else None for c in range(TILE)]
            for r in range(TILE)
        ]
        inverse = [None] * TILE
        for k in range(TILE):
            inverse[k] = 1.0 / pivot[k][k]
            scaled = jnp.where(lanes == base + k, 1.0, rows[k])
            for i in range(k + 1, TILE):
                factor = pivot[k][i] * inverse[k]
                for c in range(i, TILE):
                    pivot[i][c] = pivot[i][c] - factor * pivot[k][c]
                rows[i] = jnp.where(lanes == base + k, 0.0, rows[i]) - factor * scaled
        solved = [None] * TILE
        for k in reversed(range(TILE)):
            value = jnp.where(lanes == base + k, 1.0, rows[k])
            value = jnp.where((lanes > base + k) & (lanes < base + TILE), 0.0, value)
            for c in range(k + 1, TILE):
                value = value - pivot[k][c] * solved[c]
            solved[k] = value * inverse[k]
        wide = [jnp.broadcast_to(row, (TILE, ROWS)) for row in solved]
        inside = (lane >= base) & (lane < base + TILE)
        for t in range(at + 1, TILES):
            value = jnp.where(inside, 0.0, tiles[t])
            for k in range(TILE):
                value = value - tiles[t][:, base + k:base + k + 1] * wide[k]
            tiles[t] = value
        done = jnp.broadcast_to(rows[0], (TILE, ROWS))
        for r in range(1, TILE):
            done = jnp.where(sub == r, rows[r], done)
        tiles[at] = done
    out = []
    for t in range(TILES):
        diagonal = lane == sub + t * TILE
        square = jnp.sum(jnp.where(diagonal, tiles[t], 0.0), axis=1, keepdims=True)
        lower = jnp.where(lane < sub + t * TILE, tiles[t], jnp.where(diagonal, 1.0, 0.0))
        out.append(lower * lax.rsqrt(square))
    return jnp.concatenate(out, 0)


def cut_kernel(samples_ref, pieces_ref):
    width = pieces_ref.shape[2]
    for s in range(SAMP):
        pieces_ref[s] = samples_ref[:, s * width:(s + 1) * width]


def cut(samples):
    shape = (SAMP, ROWS, samples.shape[1] // SAMP)
    return pl.pallas_call(
        cut_kernel,
        out_shape=jax.ShapeDtypeStruct(shape, samples.dtype),
        compiler_params=pltpu.CompilerParams(vmem_limit_bytes=16 << 20),
        cost_estimate=pl.CostEstimate(flops=0, bytes_accessed=4 << 20, transcendentals=0),
    )(samples)


GROUP = 4


def gram_kernel(panel_index_ref, panel_ref, pieces_ref, *rest):
    total_ref = rest[-1]
    step = pl.program_id(0)
    for i in range(GROUP):
        product = lax.dot_general(
            panel_ref[0], pieces_ref[i], (((1,), (1,)), ((), ())), preferred_element_type=jnp.float32
        ).reshape(TILES, TILE, ROWS)
        if len(rest) == 2:
            product = product + rest[0][:, i]
        total_ref[:, i] = product


def partial_gram(panel, pieces, *received):
    width = pieces.shape[2]
    part = pl.BlockSpec((TILES, GROUP, TILE, ROWS), lambda i, panel: (0, i, 0, 0))
    return pl.pallas_call(
        gram_kernel,
        out_shape=jax.ShapeDtypeStruct((TILES, SAMP, TILE, ROWS), jnp.float32),
        grid_spec=pltpu.PrefetchScalarGridSpec(
            num_scalar_prefetch=1,
            grid=(SAMP // GROUP,),
            in_specs=[
                pl.BlockSpec((1, ROWS, width), lambda i, panel: (panel[0], 0, 0)),
                pl.BlockSpec((GROUP, ROWS, width), lambda i, panel: (i, 0, 0)),
            ] + [part] * len(received),
            out_specs=part,
        ),
        compiler_params=pltpu.CompilerParams(vmem_limit_bytes=24 << 20),
        cost_estimate=pl.CostEstimate(flops=1 << 28, bytes_accessed=4 << 20, transcendentals=0),
    )(panel[None], pieces, pieces, *received)


def factor_kernel(core_ref, mine_ref, theirs_ref, out_ref):
    even = core_ref[0] == 0

    def item(k, i):
        mine = mine_ref[:, i].reshape(ROWS, ROWS)
        theirs = theirs_ref[:, i].reshape(ROWS, ROWS)
        return jnp.where(even == (k == 0), mine, theirs)

    first = inverse_factor(item(0, 1))
    remote = exact(first, item(0, 2), ((1,), (0,)))
    second = inverse_factor(item(1, 2) - exact(remote, remote, ((0,), (0,))))
    zero = exact(first, item(0, 0), ((1,), (0,)))
    rest = item(1, 0) - exact(remote, zero, ((0,), (0,)))
    out_ref[:, :ROWS] = zero.T
    out_ref[:, ROWS:] = exact(second, rest, ((1,), (0,))).T


def factor(core, mine, theirs):
    vmem = pl.BlockSpec(memory_space=pltpu.VMEM)
    return pl.pallas_call(
        factor_kernel,
        out_shape=jax.ShapeDtypeStruct((ROWS, 2 * ROWS), jnp.float32),
        in_specs=[pl.BlockSpec(memory_space=pltpu.SMEM)] + [vmem] * 2,
        out_specs=vmem,
        compiler_params=pltpu.CompilerParams(vmem_limit_bytes=16 << 20),
        cost_estimate=pl.CostEstimate(flops=64 << 20, bytes_accessed=1 << 20, transcendentals=0),
    )(core[None], mine, theirs)


def swap_cores(block):
    return lax.ppermute(block, "par", [(i, i ^ 1) for i in range(PAR)])


def over_chips(block):
    return lax.all_to_all(block, "par", 0, 0, axis_index_groups=CHIPS_BY_CORE, tiled=True)


def per_device(samples, shift, panel_ids):
    here = lax.axis_index("samp")
    place = lax.axis_index("par")
    core = lax.rem(place, 2)
    chip = lax.div(place, 2)
    mine = jnp.where(core == 0, panel_ids[0], panel_ids[1])
    theirs = jnp.where(core == 0, panel_ids[1], panel_ids[0])

    pieces = lax.all_to_all(cut(samples), "samp", 0, 0, tiled=True)

    received = swap_cores(partial_gram(theirs, pieces))
    total = partial_gram(mine, pieces, received)

    total = over_chips(total).sum(0)
    lane = lax.broadcasted_iota(jnp.int32, (SAMP, TILE, ROWS), 2)
    sub = lax.broadcasted_iota(jnp.int32, (SAMP, TILE, ROWS), 1)
    block = lax.broadcasted_iota(jnp.int32, (SAMP, TILE, ROWS), 0)
    shifted = (lane == sub + chip * TILE) & (block == here) & (mine == here)
    total = total + jnp.where(shifted, shift[None, None, :], 0.0)

    def rows_of(k):
        rows = lax.dynamic_index_in_dim(total, panel_ids[k], 0, keepdims=True)
        return jnp.broadcast_to(rows, total.shape)

    three = jnp.stack([total, rows_of(0), rows_of(1)], 1)
    three = lax.all_to_all(three, "samp", 0, 0, tiled=True).sum(0)

    gathered = over_chips(jnp.broadcast_to(three[None], (CHIPS,) + three.shape))
    return factor(core, gathered, swap_cores(gathered))


def solution(mesh):
    placed = (P("samp", "par"), P("samp"), P())
    return jax.shard_map(
        per_device, mesh=mesh, in_specs=placed, out_specs=P("samp", None), check_vma=False
    )
```

```python
import jax
import jax.numpy as jnp
from jax import lax
from jax.experimental import pallas as pl
from jax.experimental.pallas import tpu as pltpu
from jax.sharding import PartitionSpec as P

ROWS = 128
SAMP = 16
PAR = 32
CHIPS = PAR // 2
TILE = 8
TILES = ROWS // TILE
HIGHEST = lax.Precision.HIGHEST

OVER_CHIPS = [[[s * PAR + 2 * x + c for x in range(CHIPS)] for s in range(SAMP)] for c in range(2)]
OVER_SAMP = [[[s * PAR + 2 * x + c for s in range(SAMP)] for x in range(CHIPS)] for c in range(2)]
CHIPS_THEN_SAMP = OVER_CHIPS[0] + OVER_SAMP[1]
SAMP_THEN_CHIPS = OVER_SAMP[0] + OVER_CHIPS[1]
CHIPS_BY_CORE = [[2 * x + c for x in range(CHIPS)] for c in range(2)]


def exact(left, right, contract):
    return lax.dot_general(
        left, right, (contract, ((), ())),
        precision=HIGHEST, preferred_element_type=jnp.float32,
    )


def inverse_factor(matrix):
    lane = lax.broadcasted_iota(jnp.int32, (TILE, ROWS), 1)
    sub = lax.broadcasted_iota(jnp.int32, (TILE, ROWS), 0)
    lanes = lane[:1]
    tiles = [matrix[t * TILE:(t + 1) * TILE] for t in range(TILES)]
    for at in range(TILES):
        base = at * TILE
        rows = [tiles[at][r:r + 1] for r in range(TILE)]
        pivot = [
            [jnp.broadcast_to(rows[r][:, base + c:base + c + 1], (1, ROWS)) if c >= r else None for c in range(TILE)]
            for r in range(TILE)
        ]
        inverse = [None] * TILE
        for k in range(TILE):
            inverse[k] = 1.0 / pivot[k][k]
            scaled = jnp.where(lanes == base + k, 1.0, rows[k])
            for i in range(k + 1, TILE):
                factor = pivot[k][i] * inverse[k]
                for c in range(i, TILE):
                    pivot[i][c] = pivot[i][c] - factor * pivot[k][c]
                rows[i] = jnp.where(lanes == base + k, 0.0, rows[i]) - factor * scaled
        solved = [None] * TILE
        for k in reversed(range(TILE)):
            value = jnp.where(lanes == base + k, 1.0, rows[k])
            value = jnp.where((lanes > base + k) & (lanes < base + TILE), 0.0, value)
            for c in range(k + 1, TILE):
                value = value - pivot[k][c] * solved[c]
            solved[k] = value * inverse[k]
        wide = [jnp.broadcast_to(row, (TILE, ROWS)) for row in solved]
        inside = (lane >= base) & (lane < base + TILE)
        for t in range(at + 1, TILES):
            value = jnp.where(inside, 0.0, tiles[t])
            for k in range(TILE):
                value = value - tiles[t][:, base + k:base + k + 1] * wide[k]
            tiles[t] = value
        done = jnp.broadcast_to(rows[0], (TILE, ROWS))
        for r in range(1, TILE):
            done = jnp.where(sub == r, rows[r], done)
        tiles[at] = done
    out = []
    for t in range(TILES):
        diagonal = lane == sub + t * TILE
        square = jnp.sum(jnp.where(diagonal, tiles[t], 0.0), axis=1, keepdims=True)
        lower = jnp.where(lane < sub + t * TILE, tiles[t], jnp.where(diagonal, 1.0, 0.0))
        out.append(lower * lax.rsqrt(square))
    return jnp.concatenate(out, 0)


def cut_kernel(samples_ref, pieces_ref, sems):
    width = pieces_ref.shape[2]
    copies = [
        pltpu.make_async_copy(
            samples_ref.at[:, s * width:(s + 1) * width], pieces_ref.at[s], sems.at[s]
        )
        for s in range(SAMP)
    ]
    for copy in copies:
        copy.start()
    for copy in copies:
        copy.wait()


def cut(samples):
    shape = (SAMP, ROWS, samples.shape[1] // SAMP)
    return pl.pallas_call(
        cut_kernel,
        out_shape=jax.ShapeDtypeStruct(shape, samples.dtype),
        in_specs=[pl.BlockSpec(memory_space=pl.ANY)],
        out_specs=pl.BlockSpec(memory_space=pl.ANY),
        scratch_shapes=[pltpu.SemaphoreType.DMA((SAMP,))],
        cost_estimate=pl.CostEstimate(flops=0, bytes_accessed=4 << 20, transcendentals=0),
    )(samples)


GROUP = 4


def gram_kernel(order_ref, panel_ref, pieces_ref, total_ref):
    step = pl.program_id(0)
    for i in range(GROUP):
        block = step * GROUP + i
        product = lax.dot_general(
            panel_ref[0], pieces_ref[i], (((1,), (1,)), ((), ())), preferred_element_type=jnp.float32
        ).reshape(TILES, TILE, ROWS)

        @pl.when(order_ref[1] == 0)
        def _(product=product, block=block):
            total_ref[:, block] = product

        @pl.when(order_ref[1] == 1)
        def _(product=product, block=block):
            total_ref[block] = product


def partial_gram(panel, order, pieces):
    width = pieces.shape[2]
    whole = (TILES, SAMP, TILE, ROWS)
    return pl.pallas_call(
        gram_kernel,
        out_shape=jax.ShapeDtypeStruct(whole, jnp.float32),
        grid_spec=pltpu.PrefetchScalarGridSpec(
            num_scalar_prefetch=1,
            grid=(SAMP // GROUP,),
            in_specs=[
                pl.BlockSpec((1, ROWS, width), lambda i, order: (order[0], 0, 0)),
                pl.BlockSpec((GROUP, ROWS, width), lambda i, order: (i, 0, 0)),
            ],
            out_specs=pl.BlockSpec(whole, lambda i, order: (0, 0, 0, 0)),
        ),
        compiler_params=pltpu.CompilerParams(vmem_limit_bytes=24 << 20),
        cost_estimate=pl.CostEstimate(flops=1 << 28, bytes_accessed=4 << 20, transcendentals=0),
    )(jnp.stack([panel, order]), pieces, pieces)


def inverse_kernel(block_ref, inverse_ref):
    inverse_ref[...] = inverse_factor(block_ref[...])


def first_factor(block):
    return pl.pallas_call(
        inverse_kernel,
        out_shape=jax.ShapeDtypeStruct((ROWS, ROWS), jnp.float32),
        cost_estimate=pl.CostEstimate(flops=20 << 20, bytes_accessed=1 << 20, transcendentals=0),
    )(block)


def last_kernel(flag_ref, mine_ref, theirs_ref, shift_ref, inverse_ref, other_ref, out_ref):
    row = lax.broadcasted_iota(jnp.int32, (ROWS, ROWS), 0)
    column = lax.broadcasted_iota(jnp.int32, (ROWS, ROWS), 1)
    even = flag_ref[2] == 0

    def item(k, i):
        mine = mine_ref[:, i].reshape(ROWS, ROWS)
        theirs = theirs_ref[:, i].reshape(ROWS, ROWS)
        return jnp.where(even == (k == 0), mine, theirs)

    def own(k):
        add = (row == column) & (flag_ref[k] == 1)
        return item(k, 0) + jnp.where(add, shift_ref[...], 0.0)

    inverse = inverse_ref[...]
    remote = exact(inverse, item(0, 1), ((1,), (0,)))
    second = inverse_factor(other_ref[...] - exact(remote, remote, ((0,), (0,))))
    zero = exact(inverse, own(0), ((1,), (0,)))
    rest = own(1) - exact(remote, zero, ((0,), (0,)))
    out_ref[:, :ROWS] = zero.T
    out_ref[:, ROWS:] = exact(second, rest, ((1,), (0,))).T


def last_factor(flags, mine, theirs, shift, inverse, other):
    vmem = pl.BlockSpec(memory_space=pltpu.VMEM)
    return pl.pallas_call(
        last_kernel,
        out_shape=jax.ShapeDtypeStruct((ROWS, 2 * ROWS), jnp.float32),
        in_specs=[pl.BlockSpec(memory_space=pltpu.SMEM)] + [vmem] * 5,
        out_specs=vmem,
        compiler_params=pltpu.CompilerParams(vmem_limit_bytes=16 << 20),
        cost_estimate=pl.CostEstimate(flops=64 << 20, bytes_accessed=1 << 20, transcendentals=0),
    )(flags, mine, theirs, shift, inverse, other)


def flip(block, axis, bit):
    size = SAMP if axis == "samp" else PAR
    return lax.ppermute(block, axis, [(i, i ^ bit) for i in range(size)])


def per_device(samples, shift, panel_ids):
    here = lax.axis_index("samp")
    place = lax.axis_index("par")
    core = lax.rem(place, 2)
    mine = jnp.where(core == 0, panel_ids[0], panel_ids[1])
    theirs = jnp.where(core == 0, panel_ids[1], panel_ids[0])
    axes = ("samp", "par")

    pieces = lax.all_to_all(cut(samples), "samp", 0, 0, tiled=True)

    square = lax.dot_general(
        samples, samples, (((1,), (1,)), ((), ())), preferred_element_type=jnp.float32
    )
    for bit in (1, 16, 2, 4, 8):
        square = square + flip(square, "par", bit)
    square = square + jnp.eye(ROWS, dtype=jnp.float32) * shift[:, None]
    away = here ^ mine
    for bit in (1, 2, 4):
        square = jnp.where((away & (2 * bit - 1)) < bit, square, flip(square, "samp", bit))
    pieces, square = lax.optimization_barrier((pieces, square))

    sent = flip(partial_gram(theirs, 1 - core, pieces), "par", 1)
    total = partial_gram(mine, core, pieces) + sent

    total = lax.all_to_all(total, axes, 0, 0, axis_index_groups=CHIPS_THEN_SAMP, tiled=True).sum(0)
    square = jnp.where(away < 8, square, flip(square, "samp", 8))
    swapped = flip(square, "par", 1)
    total, square, swapped = lax.optimization_barrier((total, square, swapped))
    inverse = first_factor(jnp.where(core == 0, square, swapped))
    other = jnp.where(core == 0, swapped, square)

    remote = lax.dynamic_index_in_dim(total, panel_ids[1], 0, keepdims=True)
    total = jnp.stack([total, jnp.broadcast_to(remote, total.shape)], 1)
    total = lax.all_to_all(total, axes, 0, 0, axis_index_groups=SAMP_THEN_CHIPS, tiled=True).sum(0)
    total, inverse = lax.optimization_barrier((total, inverse))

    copies = jnp.broadcast_to(total[None], (CHIPS,) + total.shape)
    gathered = lax.all_to_all(copies, "par", 0, 0, axis_index_groups=CHIPS_BY_CORE, tiled=True)
    flags = jnp.stack([panel_ids[0] == here, panel_ids[1] == here, core == 1]).astype(jnp.int32)
    return last_factor(flags, gathered, flip(gathered, "par", 1), shift[None, :], inverse, other)


def solution(mesh):
    placed = (P("samp", "par"), P("samp"), P())
    return jax.shard_map(
        per_device, mesh=mesh, in_specs=placed, out_specs=P("samp", None), check_vma=False
    )
```

```python
import jax
import jax.numpy as jnp
from jax import lax
from jax.experimental import pallas as pl
from jax.experimental.pallas import tpu as pltpu
from jax.sharding import PartitionSpec as P

ROWS = 128
SAMP = 16
PAR = 32
CHIPS = PAR // 2
TILE = 8
TILES = ROWS // TILE
HIGHEST = lax.Precision.HIGHEST

OVER_CHIPS = [[[s * PAR + 2 * x + c for x in range(CHIPS)] for s in range(SAMP)] for c in range(2)]
OVER_SAMP = [[[s * PAR + 2 * x + c for s in range(SAMP)] for x in range(CHIPS)] for c in range(2)]
CHIPS_THEN_SAMP = OVER_CHIPS[0] + OVER_SAMP[1]
SAMP_THEN_CHIPS = OVER_SAMP[0] + OVER_CHIPS[1]
CHIPS_BY_CORE = [[2 * x + c for x in range(CHIPS)] for c in range(2)]


def exact(left, right, contract):
    return lax.dot_general(
        left, right, (contract, ((), ())),
        precision=HIGHEST, preferred_element_type=jnp.float32,
    )


def inverse_factor(matrix):
    lane = lax.broadcasted_iota(jnp.int32, (TILE, ROWS), 1)
    sub = lax.broadcasted_iota(jnp.int32, (TILE, ROWS), 0)
    lanes = lane[:1]
    tiles = [matrix[t * TILE:(t + 1) * TILE] for t in range(TILES)]
    for at in range(TILES):
        base = at * TILE
        rows = [tiles[at][r:r + 1] for r in range(TILE)]
        pivot = [
            [jnp.broadcast_to(rows[r][:, base + c:base + c + 1], (1, ROWS)) if c >= r else None for c in range(TILE)]
            for r in range(TILE)
        ]
        inverse = [None] * TILE
        for k in range(TILE):
            inverse[k] = 1.0 / pivot[k][k]
            scaled = jnp.where(lanes == base + k, 1.0, rows[k])
            for i in range(k + 1, TILE):
                factor = pivot[k][i] * inverse[k]
                for c in range(i, TILE):
                    pivot[i][c] = pivot[i][c] - factor * pivot[k][c]
                rows[i] = jnp.where(lanes == base + k, 0.0, rows[i]) - factor * scaled
        solved = [None] * TILE
        for k in reversed(range(TILE)):
            value = jnp.where(lanes == base + k, 1.0, rows[k])
            value = jnp.where((lanes > base + k) & (lanes < base + TILE), 0.0, value)
            for c in range(k + 1, TILE):
                value = value - pivot[k][c] * solved[c]
            solved[k] = value * inverse[k]
        wide = [jnp.broadcast_to(row, (TILE, ROWS)) for row in solved]
        inside = (lane >= base) & (lane < base + TILE)
        for t in range(at + 1, TILES):
            value = jnp.where(inside, 0.0, tiles[t])
            for k in range(TILE):
                value = value - tiles[t][:, base + k:base + k + 1] * wide[k]
            tiles[t] = value
        done = jnp.broadcast_to(rows[0], (TILE, ROWS))
        for r in range(1, TILE):
            done = jnp.where(sub == r, rows[r], done)
        tiles[at] = done
    out = []
    for t in range(TILES):
        diagonal = lane == sub + t * TILE
        square = jnp.sum(jnp.where(diagonal, tiles[t], 0.0), axis=1, keepdims=True)
        lower = jnp.where(lane < sub + t * TILE, tiles[t], jnp.where(diagonal, 1.0, 0.0))
        out.append(lower * lax.rsqrt(square))
    return jnp.concatenate(out, 0)


def cut_kernel(samples_ref, pieces_ref, held, arrived, left):
    width = pieces_ref.shape[2]
    into = [
        pltpu.make_async_copy(samples_ref.at[:, s * width:(s + 1) * width], held.at[s], arrived.at[s])
        for s in range(SAMP)
    ]
    out = [pltpu.make_async_copy(held.at[s], pieces_ref.at[s], left.at[s]) for s in range(SAMP)]
    for copy in into:
        copy.start()
    for s in range(SAMP):
        into[s].wait()
        out[s].start()
    for copy in out:
        copy.wait()


def cut(samples):
    shape = (SAMP, ROWS, samples.shape[1] // SAMP)
    return pl.pallas_call(
        cut_kernel,
        out_shape=jax.ShapeDtypeStruct(shape, samples.dtype),
        in_specs=[pl.BlockSpec(memory_space=pl.ANY)],
        out_specs=pl.BlockSpec(memory_space=pl.ANY),
        scratch_shapes=[
            pltpu.VMEM(shape, samples.dtype),
            pltpu.SemaphoreType.DMA((SAMP,)),
            pltpu.SemaphoreType.DMA((SAMP,)),
        ],
        cost_estimate=pl.CostEstimate(flops=0, bytes_accessed=4 << 20, transcendentals=0),
    )(samples)


def gram_kernel(panel_ref, pieces_ref, total_ref):
    panel = pieces_ref[panel_ref[0]]
    for block in range(SAMP):
        total_ref[:, block] = lax.dot_general(
            panel, pieces_ref[block], (((1,), (1,)), ((), ())), preferred_element_type=jnp.float32
        ).reshape(TILES, TILE, ROWS)


VMEM = pl.BlockSpec(memory_space=pltpu.VMEM)
SMEM = pl.BlockSpec(memory_space=pltpu.SMEM)


def partial_gram(panel, pieces):
    return pl.pallas_call(
        gram_kernel,
        out_shape=jax.ShapeDtypeStruct((TILES, SAMP, TILE, ROWS), jnp.float32),
        in_specs=[SMEM, VMEM],
        out_specs=VMEM,
        compiler_params=pltpu.CompilerParams(vmem_limit_bytes=16 << 20),
        cost_estimate=pl.CostEstimate(flops=1 << 28, bytes_accessed=4 << 20, transcendentals=0),
    )(panel[None], pieces)


def join_kernel(core_ref, mine_ref, theirs_ref, strip_ref, out_ref):
    for block in range(SAMP):
        value = mine_ref[:, block] + theirs_ref[:, block]

        @pl.when(core_ref[0] == 0)
        def _(value=value, block=block):
            out_ref[:, block] = value

        @pl.when(core_ref[0] == 1)
        def _(value=value, block=block):
            out_ref[block, :SAMP] = value

        out_ref[block, SAMP] = strip_ref[...]


def join(core, mine, theirs, strip):
    return pl.pallas_call(
        join_kernel,
        out_shape=jax.ShapeDtypeStruct((TILES, SAMP + 1, TILE, ROWS), jnp.float32),
        in_specs=[SMEM, VMEM, VMEM, VMEM],
        out_specs=VMEM,
        compiler_params=pltpu.CompilerParams(vmem_limit_bytes=16 << 20),
        cost_estimate=pl.CostEstimate(flops=1 << 20, bytes_accessed=4 << 20, transcendentals=0),
    )(core[None], mine, theirs, strip)


def first_kernel(core_ref, mine_ref, theirs_ref, inverse_ref, other_ref):
    def item(i):
        mine = mine_ref[:, i].reshape(ROWS, ROWS)
        theirs = theirs_ref[:, i].reshape(ROWS, ROWS)
        return jnp.where(core_ref[0] == 1, mine, theirs)

    inverse_ref[...] = inverse_factor(item(0))
    other_ref[...] = item(1)


def first_factor(core, mine, theirs):
    square = jax.ShapeDtypeStruct((ROWS, ROWS), jnp.float32)
    return pl.pallas_call(
        first_kernel,
        out_shape=(square, square),
        in_specs=[SMEM, VMEM, VMEM],
        out_specs=(VMEM, VMEM),
        compiler_params=pltpu.CompilerParams(vmem_limit_bytes=16 << 20),
        cost_estimate=pl.CostEstimate(flops=20 << 20, bytes_accessed=1 << 20, transcendentals=0),
    )(core[None], mine, theirs)


def last_kernel(owns_ref, strips_ref, shift_ref, inverse_ref, other_ref, out_ref):
    row = lax.broadcasted_iota(jnp.int32, (ROWS, ROWS), 0)
    column = lax.broadcasted_iota(jnp.int32, (ROWS, ROWS), 1)

    def own(k):
        add = (row == column) & (owns_ref[k] == 1)
        return strips_ref[:, k, 0].reshape(ROWS, ROWS) + jnp.where(add, shift_ref[...], 0.0)

    inverse = inverse_ref[...]
    remote = exact(inverse, strips_ref[:, 0, 1].reshape(ROWS, ROWS), ((1,), (0,)))
    second = inverse_factor(other_ref[...] - exact(remote, remote, ((0,), (0,))))
    zero = exact(inverse, own(0), ((1,), (0,)))
    rest = own(1) - exact(remote, zero, ((0,), (0,)))
    out_ref[:, :ROWS] = zero.T
    out_ref[:, ROWS:] = exact(second, rest, ((1,), (0,))).T


def last_factor(owns, strips, shift, inverse, other):
    return pl.pallas_call(
        last_kernel,
        out_shape=jax.ShapeDtypeStruct((ROWS, 2 * ROWS), jnp.float32),
        in_specs=[SMEM] + [VMEM] * 4,
        out_specs=VMEM,
        compiler_params=pltpu.CompilerParams(vmem_limit_bytes=16 << 20),
        cost_estimate=pl.CostEstimate(flops=64 << 20, bytes_accessed=1 << 20, transcendentals=0),
    )(owns, strips, shift, inverse, other)


def flip(block, bit):
    return lax.ppermute(block, "par", [(i, i ^ bit) for i in range(PAR)])


def per_device(samples, shift, panel_ids):
    here = lax.axis_index("samp")
    place = lax.axis_index("par")
    core = lax.rem(place, 2)
    chip = lax.div(place, 2)
    mine = jnp.where(core == 0, panel_ids[0], panel_ids[1])
    theirs = jnp.where(core == 0, panel_ids[1], panel_ids[0])
    axes = ("samp", "par")

    pieces = lax.all_to_all(cut(samples), "samp", 0, 0, tiled=True)

    square = lax.dot_general(
        samples, samples, (((1,), (1,)), ((), ())), preferred_element_type=jnp.float32
    )
    for bit in (1, 16, 2, 4, 8):
        square = square + flip(square, bit)
    square = square + jnp.eye(ROWS, dtype=jnp.float32) * shift[:, None]
    strip = lax.dynamic_slice_in_dim(square, chip * TILE, TILE, 0)
    pieces, strip = lax.optimization_barrier((pieces, strip))

    sent = flip(partial_gram(theirs, pieces), 1)
    total = join(core, partial_gram(mine, pieces), sent, strip)

    total = lax.all_to_all(total, axes, 0, 0, axis_index_groups=CHIPS_THEN_SAMP, tiled=True)
    strips = total[:, SAMP]
    total = total[:, :SAMP].sum(0)

    def pick(array, k):
        return lax.dynamic_index_in_dim(array, panel_ids[k], 0, keepdims=False)

    one = jnp.where(core == 0, pick(total, 1), pick(strips, 0))
    two = pick(strips, 1)
    total = jnp.stack([total, jnp.broadcast_to(one, total.shape), jnp.broadcast_to(two, total.shape)], 1)
    total = lax.all_to_all(total, axes, 0, 0, axis_index_groups=SAMP_THEN_CHIPS, tiled=True)
    blocks = total[:, 1:]
    total = total[:, :2].sum(0)

    copies = jnp.broadcast_to(total[None], (PAR,) + total.shape)
    gathered = lax.all_to_all(copies, "par", 0, 0, tiled=True)
    inverse, other = first_factor(core, blocks, flip(blocks, 1))
    owns = jnp.stack([panel_ids[0] == here, panel_ids[1] == here]).astype(jnp.int32)
    gathered = gathered.reshape(CHIPS, 2, 2, TILE, ROWS)
    return last_factor(owns, gathered, shift[None, :], inverse, other)


def solution(mesh):
    placed = (P("samp", "par"), P("samp"), P())
    return jax.shard_map(
        per_device, mesh=mesh, in_specs=placed, out_specs=P("samp", None), check_vma=False
    )
```

```python
import jax
import jax.numpy as jnp
from jax import lax
from jax.experimental import pallas as pl
from jax.experimental.pallas import tpu as pltpu
from jax.sharding import PartitionSpec as P

ROWS = 128
SAMP = 16
PAR = 32
CHIPS = PAR // 2
TILE = 8
TILES = ROWS // TILE
HIGHEST = lax.Precision.HIGHEST

OVER_CHIPS = [[[s * PAR + 2 * x + c for x in range(CHIPS)] for s in range(SAMP)] for c in range(2)]
OVER_SAMP = [[[s * PAR + 2 * x + c for s in range(SAMP)] for x in range(CHIPS)] for c in range(2)]
CHIPS_THEN_SAMP = OVER_CHIPS[0] + OVER_SAMP[1]
SAMP_THEN_CHIPS = OVER_SAMP[0] + OVER_CHIPS[1]
CHIPS_BY_CORE = [[2 * x + c for x in range(CHIPS)] for c in range(2)]


def exact(left, right, contract):
    return lax.dot_general(
        left, right, (contract, ((), ())),
        precision=HIGHEST, preferred_element_type=jnp.float32,
    )


def inverse_factor(matrix):
    lane = lax.broadcasted_iota(jnp.int32, (TILE, ROWS), 1)
    sub = lax.broadcasted_iota(jnp.int32, (TILE, ROWS), 0)
    lanes = lane[:1]
    tiles = [matrix[t * TILE:(t + 1) * TILE] for t in range(TILES)]
    for at in range(TILES):
        base = at * TILE
        rows = [tiles[at][r:r + 1] for r in range(TILE)]
        pivot = [
            [jnp.broadcast_to(rows[r][:, base + c:base + c + 1], (1, ROWS)) if c >= r else None for c in range(TILE)]
            for r in range(TILE)
        ]
        inverse = [None] * TILE
        for k in range(TILE):
            inverse[k] = 1.0 / pivot[k][k]
            scaled = jnp.where(lanes == base + k, 1.0, rows[k])
            for i in range(k + 1, TILE):
                factor = pivot[k][i] * inverse[k]
                for c in range(i, TILE):
                    pivot[i][c] = pivot[i][c] - factor * pivot[k][c]
                rows[i] = jnp.where(lanes == base + k, 0.0, rows[i]) - factor * scaled
        solved = [None] * TILE
        for k in reversed(range(TILE)):
            value = jnp.where(lanes == base + k, 1.0, rows[k])
            value = jnp.where((lanes > base + k) & (lanes < base + TILE), 0.0, value)
            for c in range(TILE - 1, k, -1):
                value = value - pivot[k][c] * solved[c]
            solved[k] = value * inverse[k]
        wide = [jnp.broadcast_to(row, (TILE, ROWS)) for row in solved]
        inside = (lane >= base) & (lane < base + TILE)
        for t in range(at + 1, TILES):
            value = jnp.where(inside, 0.0, tiles[t])
            for k in reversed(range(TILE)):
                value = value - tiles[t][:, base + k:base + k + 1] * wide[k]
            tiles[t] = value
        done = None
        for r in range(TILE):
            row = jnp.where(lanes < base + r, rows[r], jnp.where(lanes == base + r, 1.0, 0.0))
            row = jnp.broadcast_to(row * lax.rsqrt(pivot[r][r]), (TILE, ROWS))
            done = row if done is None else jnp.where(sub == r, row, done)
        tiles[at] = done
    return jnp.concatenate(tiles, 0)


def cut_kernel(samples_ref, pieces_ref, held, arrived, left):
    width = pieces_ref.shape[2]
    into = [
        pltpu.make_async_copy(samples_ref.at[:, s * width:(s + 1) * width], held.at[s], arrived.at[s])
        for s in range(SAMP)
    ]
    out = [pltpu.make_async_copy(held.at[s], pieces_ref.at[s], left.at[s]) for s in range(SAMP)]
    for copy in into:
        copy.start()
    for s in range(SAMP):
        into[s].wait()
        out[s].start()
    for copy in out:
        copy.wait()


def cut(samples):
    shape = (SAMP, ROWS, samples.shape[1] // SAMP)
    return pl.pallas_call(
        cut_kernel,
        out_shape=jax.ShapeDtypeStruct(shape, samples.dtype),
        in_specs=[pl.BlockSpec(memory_space=pl.ANY)],
        out_specs=pl.BlockSpec(memory_space=pl.ANY),
        scratch_shapes=[
            pltpu.VMEM(shape, samples.dtype),
            pltpu.SemaphoreType.DMA((SAMP,)),
            pltpu.SemaphoreType.DMA((SAMP,)),
        ],
        cost_estimate=pl.CostEstimate(flops=0, bytes_accessed=4 << 20, transcendentals=0),
    )(samples)


def gram_kernel(panel_ref, pieces_ref, total_ref):
    panel = pieces_ref[panel_ref[0]]
    for block in range(SAMP):
        total_ref[:, block] = lax.dot_general(
            panel, pieces_ref[block], (((1,), (1,)), ((), ())), preferred_element_type=jnp.float32
        ).reshape(TILES, TILE, ROWS)


VMEM = pl.BlockSpec(memory_space=pltpu.VMEM)
SMEM = pl.BlockSpec(memory_space=pltpu.SMEM)


def partial_gram(panel, pieces):
    return pl.pallas_call(
        gram_kernel,
        out_shape=jax.ShapeDtypeStruct((TILES, SAMP, TILE, ROWS), jnp.float32),
        in_specs=[SMEM, VMEM],
        out_specs=VMEM,
        compiler_params=pltpu.CompilerParams(vmem_limit_bytes=16 << 20),
        cost_estimate=pl.CostEstimate(flops=1 << 28, bytes_accessed=4 << 20, transcendentals=0),
    )(panel[None], pieces)


PART = 4


def join_kernel(core_ref, mine_ref, theirs_ref, strip_ref, out_ref, theirs_held, held, arrived, left):
    def arrival(part):
        tiles = pl.ds(part * PART, PART)
        return pltpu.make_async_copy(theirs_ref.at[tiles], theirs_held.at[tiles], arrived.at[part])

    def departure(tile, core):
        place = out_ref.at[tile, pl.ds(0, SAMP)] if core == 0 else out_ref.at[:, tile]
        return pltpu.make_async_copy(held.at[tile], place, left.at[tile])

    def strips():
        return pltpu.make_async_copy(held.at[TILES], out_ref.at[:, SAMP], left.at[TILES])

    def on_core(core, tiles, act):
        @pl.when(core_ref[0] == core)
        def _():
            for tile in tiles:
                act(departure(tile, core))

    for part in range(TILES // PART):
        arrival(part).start()
    held[TILES] = jnp.broadcast_to(strip_ref[...][None], (SAMP, TILE, ROWS))
    strips().start()
    for part in range(TILES // PART):
        arrival(part).wait()
        tiles = range(part * PART, part * PART + PART)
        for tile in tiles:
            held[tile] = mine_ref[tile] + theirs_held[tile]
        for core in range(2):
            on_core(core, tiles, lambda copy: copy.start())
    for core in range(2):
        on_core(core, range(TILES), lambda copy: copy.wait())
    strips().wait()


def join(core, mine, theirs, strip):
    anywhere = pl.BlockSpec(memory_space=pl.ANY)
    return pl.pallas_call(
        join_kernel,
        out_shape=jax.ShapeDtypeStruct((TILES, SAMP + 1, TILE, ROWS), jnp.float32),
        in_specs=[SMEM, VMEM, anywhere, VMEM],
        out_specs=anywhere,
        scratch_shapes=[
            pltpu.VMEM((TILES, SAMP, TILE, ROWS), jnp.float32),
            pltpu.VMEM((TILES + 1, SAMP, TILE, ROWS), jnp.float32),
            pltpu.SemaphoreType.DMA((TILES // PART,)),
            pltpu.SemaphoreType.DMA((TILES + 1,)),
        ],
        compiler_params=pltpu.CompilerParams(vmem_limit_bytes=16 << 20),
        cost_estimate=pl.CostEstimate(flops=1 << 20, bytes_accessed=4 << 20, transcendentals=0),
    )(core[None], mine, theirs, strip)


def first_kernel(core_ref, mine_ref, theirs_ref, inverse_ref, other_ref):
    def item(i):
        mine = mine_ref[:, i].reshape(ROWS, ROWS)
        theirs = theirs_ref[:, i].reshape(ROWS, ROWS)
        return jnp.where(core_ref[0] == 1, mine, theirs)

    inverse_ref[...] = inverse_factor(item(0))
    other_ref[...] = item(1)


def first_factor(core, mine, theirs):
    square = jax.ShapeDtypeStruct((ROWS, ROWS), jnp.float32)
    return pl.pallas_call(
        first_kernel,
        out_shape=(square, square),
        in_specs=[SMEM, VMEM, VMEM],
        out_specs=(VMEM, VMEM),
        compiler_params=pltpu.CompilerParams(vmem_limit_bytes=16 << 20),
        cost_estimate=pl.CostEstimate(flops=20 << 20, bytes_accessed=1 << 20, transcendentals=0),
    )(core[None], mine, theirs)


def last_kernel(flags_ref, mine_ref, theirs_ref, shift_ref, inverse_ref, other_ref, out_ref):
    row = lax.broadcasted_iota(jnp.int32, (ROWS, ROWS), 0)
    column = lax.broadcasted_iota(jnp.int32, (ROWS, ROWS), 1)

    def item(k, i):
        mine = mine_ref[:, i].reshape(ROWS, ROWS)
        theirs = theirs_ref[:, i].reshape(ROWS, ROWS)
        return jnp.where(flags_ref[2] == k, mine, theirs)

    def own(k):
        add = (row == column) & (flags_ref[k] == 1)
        return item(k, 0) + jnp.where(add, shift_ref[...], 0.0)

    inverse = inverse_ref[...]
    remote = exact(inverse, item(0, 1), ((1,), (0,)))
    second = inverse_factor(other_ref[...] - exact(remote, remote, ((0,), (0,))))
    zero = exact(inverse, own(0), ((1,), (0,)))
    rest = own(1) - exact(remote, zero, ((0,), (0,)))
    out_ref[:, :ROWS] = zero.T
    out_ref[:, ROWS:] = exact(second, rest, ((1,), (0,))).T


def last_factor(flags, mine, theirs, shift, inverse, other):
    return pl.pallas_call(
        last_kernel,
        out_shape=jax.ShapeDtypeStruct((ROWS, 2 * ROWS), jnp.float32),
        in_specs=[SMEM] + [VMEM] * 5,
        out_specs=VMEM,
        compiler_params=pltpu.CompilerParams(vmem_limit_bytes=16 << 20),
        cost_estimate=pl.CostEstimate(flops=64 << 20, bytes_accessed=1 << 20, transcendentals=0),
    )(flags, mine, theirs, shift, inverse, other)


def flip(block, bit):
    return lax.ppermute(block, "par", [(i, i ^ bit) for i in range(PAR)])


def per_device(samples, shift, panel_ids):
    here = lax.axis_index("samp")
    place = lax.axis_index("par")
    core = lax.rem(place, 2)
    chip = lax.div(place, 2)
    mine = jnp.where(core == 0, panel_ids[0], panel_ids[1])
    theirs = jnp.where(core == 0, panel_ids[1], panel_ids[0])
    axes = ("samp", "par")

    pieces = lax.all_to_all(cut(samples), "samp", 0, 0, tiled=True)

    square = lax.dot_general(
        samples, samples, (((1,), (1,)), ((), ())), preferred_element_type=jnp.float32
    )
    for bit in (1, 16, 2, 4, 8):
        square = square + flip(square, bit)
    square = square + jnp.eye(ROWS, dtype=jnp.float32) * shift[:, None]
    strip = lax.dynamic_slice_in_dim(square, chip * TILE, TILE, 0)
    pieces, strip = lax.optimization_barrier((pieces, strip))

    sent = flip(partial_gram(theirs, pieces), 1)
    total = join(core, partial_gram(mine, pieces), sent, strip)

    total = lax.all_to_all(total, axes, 0, 0, axis_index_groups=CHIPS_THEN_SAMP, tiled=True)
    strips = total[:, SAMP]
    total = total[:, :SAMP].sum(0)

    def pick(array, k):
        return lax.dynamic_index_in_dim(array, panel_ids[k], 0, keepdims=False)

    one = jnp.where(core == 0, pick(total, 1), pick(strips, 0))
    two = pick(strips, 1)
    total = jnp.stack([total, jnp.broadcast_to(one, total.shape), jnp.broadcast_to(two, total.shape)], 1)
    total = lax.all_to_all(total, axes, 0, 0, axis_index_groups=SAMP_THEN_CHIPS, tiled=True)
    blocks = total[:, 1:]
    total = total[:, :2].sum(0)

    copies = jnp.broadcast_to(total[None], (CHIPS,) + total.shape)
    gathered = lax.all_to_all(copies, "par", 0, 0, axis_index_groups=CHIPS_BY_CORE, tiled=True)
    inverse, other = first_factor(core, blocks, flip(blocks, 1))
    gathered, inverse = lax.optimization_barrier((gathered, inverse))
    flags = jnp.stack([
        (panel_ids[0] == here).astype(jnp.int32), (panel_ids[1] == here).astype(jnp.int32), core
    ])
    return last_factor(flags, gathered, flip(gathered, 1), shift[None, :], inverse, other)


def solution(mesh):
    placed = (P("samp", "par"), P("samp"), P())
    return jax.shard_map(
        per_device, mesh=mesh, in_specs=placed, out_specs=P("samp", None), check_vma=False
    )
```

```python
import jax
import jax.numpy as jnp
from jax import lax
from jax.experimental import pallas as pl
from jax.experimental.pallas import tpu as pltpu
from jax.sharding import PartitionSpec as P

ROWS = 128
SAMP = 16
PAR = 32
CHIPS = PAR // 2
TILE = 8
TILES = ROWS // TILE
HIGHEST = lax.Precision.HIGHEST

OVER_CHIPS = [[[s * PAR + 2 * x + c for x in range(CHIPS)] for s in range(SAMP)] for c in range(2)]
OVER_SAMP = [[[s * PAR + 2 * x + c for s in range(SAMP)] for x in range(CHIPS)] for c in range(2)]
CHIPS_THEN_SAMP = OVER_CHIPS[0] + OVER_SAMP[1]
SAMP_THEN_CHIPS = OVER_SAMP[0] + OVER_CHIPS[1]
CHIPS_BY_CORE = [[2 * x + c for x in range(CHIPS)] for c in range(2)]


def exact(left, right, contract):
    return lax.dot_general(
        left, right, (contract, ((), ())),
        precision=HIGHEST, preferred_element_type=jnp.float32,
    )


def inverse_factor(matrix):
    lane = lax.broadcasted_iota(jnp.int32, (TILE, ROWS), 1)
    sub = lax.broadcasted_iota(jnp.int32, (TILE, ROWS), 0)
    lanes = lane[:1]
    tiles = [matrix[t * TILE:(t + 1) * TILE] for t in range(TILES)]
    for at in range(TILES):
        base = at * TILE
        rows = [tiles[at][r:r + 1] for r in range(TILE)]
        pivot = [
            [jnp.broadcast_to(rows[r][:, base + c:base + c + 1], (1, ROWS)) if c >= r else None for c in range(TILE)]
            for r in range(TILE)
        ]
        inverse = [None] * TILE
        for k in range(TILE):
            inverse[k] = 1.0 / pivot[k][k]
            scaled = jnp.where(lanes == base + k, 1.0, rows[k])
            for i in range(k + 1, TILE):
                factor = pivot[k][i] * inverse[k]
                for c in range(i, TILE):
                    pivot[i][c] = pivot[i][c] - factor * pivot[k][c]
                rows[i] = jnp.where(lanes == base + k, 0.0, rows[i]) - factor * scaled
        solved = [None] * TILE
        for k in reversed(range(TILE)):
            value = jnp.where(lanes == base + k, 1.0, rows[k])
            value = jnp.where((lanes > base + k) & (lanes < base + TILE), 0.0, value)
            for c in range(TILE - 1, k, -1):
                value = value - pivot[k][c] * solved[c]
            solved[k] = value * inverse[k]
        wide = [jnp.broadcast_to(row, (TILE, ROWS)) for row in solved]
        inside = (lane >= base) & (lane < base + TILE)
        for t in range(at + 1, TILES):
            value = jnp.where(inside, 0.0, tiles[t])
            for k in reversed(range(TILE)):
                value = value - tiles[t][:, base + k:base + k + 1] * wide[k]
            tiles[t] = value
        done = None
        for r in range(TILE):
            row = jnp.where(lanes < base + r, rows[r], jnp.where(lanes == base + r, 1.0, 0.0))
            row = jnp.broadcast_to(row * lax.rsqrt(pivot[r][r]), (TILE, ROWS))
            done = row if done is None else jnp.where(sub == r, row, done)
        tiles[at] = done
    return jnp.concatenate(tiles, 0)


def cut_kernel(samples_ref, pieces_ref, held, arrived, left):
    width = pieces_ref.shape[2]
    into = [
        pltpu.make_async_copy(samples_ref.at[:, s * width:(s + 1) * width], held.at[s], arrived.at[s])
        for s in range(SAMP)
    ]
    out = [pltpu.make_async_copy(held.at[s], pieces_ref.at[s], left.at[s]) for s in range(SAMP)]
    for copy in into:
        copy.start()
    for s in range(SAMP):
        into[s].wait()
        out[s].start()
    for copy in out:
        copy.wait()


def cut(samples):
    shape = (SAMP, ROWS, samples.shape[1] // SAMP)
    return pl.pallas_call(
        cut_kernel,
        out_shape=jax.ShapeDtypeStruct(shape, samples.dtype),
        in_specs=[pl.BlockSpec(memory_space=pl.ANY)],
        out_specs=pl.BlockSpec(memory_space=pl.ANY),
        scratch_shapes=[
            pltpu.VMEM(shape, samples.dtype),
            pltpu.SemaphoreType.DMA((SAMP,)),
            pltpu.SemaphoreType.DMA((SAMP,)),
        ],
        cost_estimate=pl.CostEstimate(flops=0, bytes_accessed=4 << 20, transcendentals=0),
    )(samples)


def gram_kernel(panel_ref, pieces_ref, total_ref):
    panel = pieces_ref[panel_ref[0]]
    for block in range(SAMP):
        total_ref[:, block] = lax.dot_general(
            panel, pieces_ref[block], (((1,), (1,)), ((), ())), preferred_element_type=jnp.float32
        ).reshape(TILES, TILE, ROWS)


VMEM = pl.BlockSpec(memory_space=pltpu.VMEM)
SMEM = pl.BlockSpec(memory_space=pltpu.SMEM)


def partial_gram(panel, pieces):
    return pl.pallas_call(
        gram_kernel,
        out_shape=jax.ShapeDtypeStruct((TILES, SAMP, TILE, ROWS), jnp.float32),
        in_specs=[SMEM, VMEM],
        out_specs=VMEM,
        compiler_params=pltpu.CompilerParams(vmem_limit_bytes=16 << 20),
        cost_estimate=pl.CostEstimate(flops=1 << 28, bytes_accessed=4 << 20, transcendentals=0),
    )(panel[None], pieces)


PART = 4


def join_kernel(core_ref, mine_ref, theirs_ref, strip_ref, out_ref, theirs_held, held, arrived, left):
    def arrival(part):
        tiles = pl.ds(part * PART, PART)
        return pltpu.make_async_copy(theirs_ref.at[tiles], theirs_held.at[tiles], arrived.at[part])

    def departure(tile, core):
        place = out_ref.at[tile, pl.ds(0, SAMP)] if core == 0 else out_ref.at[:, tile]
        return pltpu.make_async_copy(held.at[tile], place, left.at[tile])

    def strips():
        return pltpu.make_async_copy(held.at[TILES], out_ref.at[:, SAMP], left.at[TILES])

    def on_core(core, tiles, act):
        @pl.when(core_ref[0] == core)
        def _():
            for tile in tiles:
                act(departure(tile, core))

    for part in range(TILES // PART):
        arrival(part).start()
    held[TILES] = jnp.broadcast_to(strip_ref[...][None], (SAMP, TILE, ROWS))
    strips().start()
    for part in range(TILES // PART):
        arrival(part).wait()
        tiles = range(part * PART, part * PART + PART)
        for tile in tiles:
            held[tile] = mine_ref[tile] + theirs_held[tile]
        for core in range(2):
            on_core(core, tiles, lambda copy: copy.start())
    for core in range(2):
        on_core(core, range(TILES), lambda copy: copy.wait())
    strips().wait()


def join(core, mine, theirs, strip):
    anywhere = pl.BlockSpec(memory_space=pl.ANY)
    return pl.pallas_call(
        join_kernel,
        out_shape=jax.ShapeDtypeStruct((TILES, SAMP + 1, TILE, ROWS), jnp.float32),
        in_specs=[SMEM, VMEM, anywhere, VMEM],
        out_specs=anywhere,
        scratch_shapes=[
            pltpu.VMEM((TILES, SAMP, TILE, ROWS), jnp.float32),
            pltpu.VMEM((TILES + 1, SAMP, TILE, ROWS), jnp.float32),
            pltpu.SemaphoreType.DMA((TILES // PART,)),
            pltpu.SemaphoreType.DMA((TILES + 1,)),
        ],
        compiler_params=pltpu.CompilerParams(vmem_limit_bytes=16 << 20),
        cost_estimate=pl.CostEstimate(flops=1 << 20, bytes_accessed=4 << 20, transcendentals=0),
    )(core[None], mine, theirs, strip)


def first_kernel(core_ref, mine_ref, theirs_ref, inverse_ref, other_ref):
    def item(i):
        mine = mine_ref[:, i].reshape(ROWS, ROWS)
        theirs = theirs_ref[:, i].reshape(ROWS, ROWS)
        return jnp.where(core_ref[0] == 1, mine, theirs)

    inverse_ref[...] = inverse_factor(item(0))
    other_ref[...] = item(1)


def first_factor(core, mine, theirs):
    square = jax.ShapeDtypeStruct((ROWS, ROWS), jnp.float32)
    return pl.pallas_call(
        first_kernel,
        out_shape=(square, square),
        in_specs=[SMEM, VMEM, VMEM],
        out_specs=(VMEM, VMEM),
        compiler_params=pltpu.CompilerParams(vmem_limit_bytes=16 << 20),
        cost_estimate=pl.CostEstimate(flops=20 << 20, bytes_accessed=1 << 20, transcendentals=0),
    )(core[None], mine, theirs)


def last_kernel(owns_ref, strips_ref, shift_ref, inverse_ref, other_ref, out_ref):
    row = lax.broadcasted_iota(jnp.int32, (ROWS, ROWS), 0)
    column = lax.broadcasted_iota(jnp.int32, (ROWS, ROWS), 1)

    def item(i):
        return strips_ref[:, i].reshape(ROWS, ROWS)

    def own(k):
        add = (row == column) & (owns_ref[k] == 1)
        return item(k) + jnp.where(add, shift_ref[...], 0.0)

    inverse = inverse_ref[...]
    remote = exact(inverse, item(2), ((1,), (0,)))
    second = inverse_factor(other_ref[...] - exact(remote, remote, ((0,), (0,))))
    zero = exact(inverse, own(0), ((1,), (0,)))
    rest = own(1) - exact(remote, zero, ((0,), (0,)))
    out_ref[:, :ROWS] = zero.T
    out_ref[:, ROWS:] = exact(second, rest, ((1,), (0,))).T


def last_factor(owns, strips, shift, inverse, other):
    return pl.pallas_call(
        last_kernel,
        out_shape=jax.ShapeDtypeStruct((ROWS, 2 * ROWS), jnp.float32),
        in_specs=[SMEM] + [VMEM] * 4,
        out_specs=VMEM,
        compiler_params=pltpu.CompilerParams(vmem_limit_bytes=16 << 20),
        cost_estimate=pl.CostEstimate(flops=64 << 20, bytes_accessed=1 << 20, transcendentals=0),
    )(owns, strips, shift, inverse, other)


def flip(block, bit):
    return lax.ppermute(block, "par", [(i, i ^ bit) for i in range(PAR)])


def per_device(samples, shift, panel_ids):
    here = lax.axis_index("samp")
    place = lax.axis_index("par")
    core = lax.rem(place, 2)
    chip = lax.div(place, 2)
    mine = jnp.where(core == 0, panel_ids[0], panel_ids[1])
    theirs = jnp.where(core == 0, panel_ids[1], panel_ids[0])
    axes = ("samp", "par")

    pieces = lax.all_to_all(cut(samples), "samp", 0, 0, tiled=True)

    square = lax.dot_general(
        samples, samples, (((1,), (1,)), ((), ())), preferred_element_type=jnp.float32
    )
    for bit in (1, 16, 2, 4, 8):
        square = square + flip(square, bit)
    square = square + jnp.eye(ROWS, dtype=jnp.float32) * shift[:, None]
    strip = lax.dynamic_slice_in_dim(square, chip * TILE, TILE, 0)
    pieces, strip = lax.optimization_barrier((pieces, strip))

    sent = flip(partial_gram(theirs, pieces), 1)
    total = join(core, partial_gram(mine, pieces), sent, strip)

    total = lax.all_to_all(total, axes, 0, 0, axis_index_groups=CHIPS_THEN_SAMP, tiled=True)
    strips = total[:, SAMP]
    total = total[:, :SAMP].sum(0)

    def pick(array, k):
        return lax.dynamic_index_in_dim(array, panel_ids[k], 0, keepdims=False)

    one = jnp.where(core == 0, pick(total, 1), pick(strips, 0))
    two = pick(strips, 1)
    total = jnp.stack([total, jnp.broadcast_to(one, total.shape), jnp.broadcast_to(two, total.shape)], 1)
    total = lax.all_to_all(total, axes, 0, 0, axis_index_groups=SAMP_THEN_CHIPS, tiled=True)
    blocks = total[:, 1:]
    total = total[:, :2].sum(0)
    across = flip(total, 1)
    three = jnp.stack([
        jnp.where(core == 0, total[0], across[0]),
        jnp.where(core == 0, across[0], total[0]),
        jnp.where(core == 0, total[1], across[1]),
    ])
    three, blocks = lax.optimization_barrier((three, blocks))

    copies = jnp.broadcast_to(three[None], (CHIPS,) + three.shape)
    strips = lax.all_to_all(copies, "par", 0, 0, axis_index_groups=CHIPS_BY_CORE, tiled=True)
    inverse, other = first_factor(core, blocks, flip(blocks, 1))
    owns = jnp.stack([panel_ids[0] == here, panel_ids[1] == here]).astype(jnp.int32)
    return last_factor(owns, strips, shift[None, :], inverse, other)


def solution(mesh):
    placed = (P("samp", "par"), P("samp"), P())
    return jax.shard_map(
        per_device, mesh=mesh, in_specs=placed, out_specs=P("samp", None), check_vma=False
    )
```

```python
import jax
import jax.numpy as jnp
from jax import lax
from jax.experimental import pallas as pl
from jax.experimental.pallas import tpu as pltpu
from jax.sharding import PartitionSpec as P

ROWS = 128
SAMP = 16
PAR = 32
CHIPS = PAR // 2
TILE = 8
TILES = ROWS // TILE
HIGHEST = lax.Precision.HIGHEST

OVER_CHIPS = [[[s * PAR + 2 * x + c for x in range(CHIPS)] for s in range(SAMP)] for c in range(2)]
OVER_SAMP = [[[s * PAR + 2 * x + c for s in range(SAMP)] for x in range(CHIPS)] for c in range(2)]
CHIPS_THEN_SAMP = OVER_CHIPS[0] + OVER_SAMP[1]
SAMP_THEN_CHIPS = OVER_SAMP[0] + OVER_CHIPS[1]
CHIPS_BY_CORE = [[2 * x + c for x in range(CHIPS)] for c in range(2)]


def exact(left, right, contract):
    return lax.dot_general(
        left, right, (contract, ((), ())),
        precision=HIGHEST, preferred_element_type=jnp.float32,
    )


def inverse_factor(matrix):
    lane = lax.broadcasted_iota(jnp.int32, (TILE, ROWS), 1)
    sub = lax.broadcasted_iota(jnp.int32, (TILE, ROWS), 0)
    lanes = lane[:1]
    tiles = [matrix[t * TILE:(t + 1) * TILE] for t in range(TILES)]
    for at in range(TILES):
        base = at * TILE
        rows = [tiles[at][r:r + 1] for r in range(TILE)]
        pivot = [
            [jnp.broadcast_to(rows[r][:, base + c:base + c + 1], (1, ROWS)) if c >= r else None for c in range(TILE)]
            for r in range(TILE)
        ]
        inverse = [None] * TILE
        for k in range(TILE):
            inverse[k] = 1.0 / pivot[k][k]
            scaled = jnp.where(lanes == base + k, 1.0, rows[k])
            for i in range(k + 1, TILE):
                factor = pivot[k][i] * inverse[k]
                for c in range(i, TILE):
                    pivot[i][c] = pivot[i][c] - factor * pivot[k][c]
                rows[i] = jnp.where(lanes == base + k, 0.0, rows[i]) - factor * scaled
        solved = [None] * TILE
        for k in reversed(range(TILE)):
            value = jnp.where(lanes == base + k, 1.0, rows[k])
            value = jnp.where((lanes > base + k) & (lanes < base + TILE), 0.0, value)
            for c in range(TILE - 1, k, -1):
                value = value - pivot[k][c] * solved[c]
            solved[k] = value * inverse[k]
        wide = [jnp.broadcast_to(row, (TILE, ROWS)) for row in solved]
        inside = (lane >= base) & (lane < base + TILE)
        for t in range(at + 1, TILES):
            value = jnp.where(inside, 0.0, tiles[t])
            for k in reversed(range(TILE)):
                value = value - tiles[t][:, base + k:base + k + 1] * wide[k]
            tiles[t] = value
        done = None
        for r in range(TILE):
            row = jnp.where(lanes < base + r, rows[r], jnp.where(lanes == base + r, 1.0, 0.0))
            row = jnp.broadcast_to(row * lax.rsqrt(pivot[r][r]), (TILE, ROWS))
            done = row if done is None else jnp.where(sub == r, row, done)
        tiles[at] = done
    return jnp.concatenate(tiles, 0)


def cut_kernel(samples_ref, pieces_ref, held, arrived, left):
    width = pieces_ref.shape[2]
    into = [
        pltpu.make_async_copy(samples_ref.at[:, s * width:(s + 1) * width], held.at[s], arrived.at[s])
        for s in range(SAMP)
    ]
    out = [pltpu.make_async_copy(held.at[s], pieces_ref.at[s], left.at[s]) for s in range(SAMP)]
    for copy in into:
        copy.start()
    for s in range(SAMP):
        into[s].wait()
        out[s].start()
    for copy in out:
        copy.wait()


def cut(samples):
    shape = (SAMP, ROWS, samples.shape[1] // SAMP)
    return pl.pallas_call(
        cut_kernel,
        out_shape=jax.ShapeDtypeStruct(shape, samples.dtype),
        in_specs=[pl.BlockSpec(memory_space=pl.ANY)],
        out_specs=pl.BlockSpec(memory_space=pl.ANY),
        scratch_shapes=[
            pltpu.VMEM(shape, samples.dtype),
            pltpu.SemaphoreType.DMA((SAMP,)),
            pltpu.SemaphoreType.DMA((SAMP,)),
        ],
        cost_estimate=pl.CostEstimate(flops=0, bytes_accessed=4 << 20, transcendentals=0),
    )(samples)


def gram_kernel(panel_ref, pieces_ref, total_ref):
    panel = pieces_ref[panel_ref[0]]
    for block in range(SAMP):
        total_ref[:, block] = lax.dot_general(
            panel, pieces_ref[block], (((1,), (1,)), ((), ())), preferred_element_type=jnp.float32
        ).reshape(TILES, TILE, ROWS)


VMEM = pl.BlockSpec(memory_space=pltpu.VMEM)
SMEM = pl.BlockSpec(memory_space=pltpu.SMEM)


def partial_gram(panel, pieces):
    return pl.pallas_call(
        gram_kernel,
        out_shape=jax.ShapeDtypeStruct((TILES, SAMP, TILE, ROWS), jnp.float32),
        in_specs=[SMEM, VMEM],
        out_specs=VMEM,
        compiler_params=pltpu.CompilerParams(vmem_limit_bytes=16 << 20),
        cost_estimate=pl.CostEstimate(flops=1 << 28, bytes_accessed=4 << 20, transcendentals=0),
    )(panel[None], pieces)


PART = 4


def join_kernel(core_ref, mine_ref, theirs_ref, strip_ref, out_ref, theirs_held, held, arrived, left):
    def arrival(part):
        tiles = pl.ds(part * PART, PART)
        return pltpu.make_async_copy(theirs_ref.at[tiles], theirs_held.at[tiles], arrived.at[part])

    def departure(tile, core):
        place = out_ref.at[tile, pl.ds(0, SAMP)] if core == 0 else out_ref.at[:, tile]
        return pltpu.make_async_copy(held.at[tile], place, left.at[tile])

    def strips():
        return pltpu.make_async_copy(held.at[TILES], out_ref.at[:, SAMP], left.at[TILES])

    def on_core(core, tiles, act):
        @pl.when(core_ref[0] == core)
        def _():
            for tile in tiles:
                act(departure(tile, core))

    for part in range(TILES // PART):
        arrival(part).start()
    held[TILES] = jnp.broadcast_to(strip_ref[...][None], (SAMP, TILE, ROWS))
    strips().start()
    for part in range(TILES // PART):
        arrival(part).wait()
        tiles = range(part * PART, part * PART + PART)
        for tile in tiles:
            held[tile] = mine_ref[tile] + theirs_held[tile]
        for core in range(2):
            on_core(core, tiles, lambda copy: copy.start())
    for core in range(2):
        on_core(core, range(TILES), lambda copy: copy.wait())
    strips().wait()


def join(core, mine, theirs, strip):
    anywhere = pl.BlockSpec(memory_space=pl.ANY)
    return pl.pallas_call(
        join_kernel,
        out_shape=jax.ShapeDtypeStruct((TILES, SAMP + 1, TILE, ROWS), jnp.float32),
        in_specs=[SMEM, VMEM, anywhere, VMEM],
        out_specs=anywhere,
        scratch_shapes=[
            pltpu.VMEM((TILES, SAMP, TILE, ROWS), jnp.float32),
            pltpu.VMEM((TILES + 1, SAMP, TILE, ROWS), jnp.float32),
            pltpu.SemaphoreType.DMA((TILES // PART,)),
            pltpu.SemaphoreType.DMA((TILES + 1,)),
        ],
        compiler_params=pltpu.CompilerParams(vmem_limit_bytes=16 << 20),
        cost_estimate=pl.CostEstimate(flops=1 << 20, bytes_accessed=4 << 20, transcendentals=0),
    )(core[None], mine, theirs, strip)


def first_kernel(blocks_ref, pair_ref):
    pair_ref[0] = inverse_factor(blocks_ref[:, 0].reshape(ROWS, ROWS))
    pair_ref[1] = blocks_ref[:, 1].reshape(ROWS, ROWS)


def first_factor(blocks):
    return pl.pallas_call(
        first_kernel,
        out_shape=jax.ShapeDtypeStruct((2, ROWS, ROWS), jnp.float32),
        in_specs=[VMEM],
        out_specs=VMEM,
        compiler_params=pltpu.CompilerParams(vmem_limit_bytes=16 << 20),
        cost_estimate=pl.CostEstimate(flops=20 << 20, bytes_accessed=1 << 20, transcendentals=0),
    )(blocks)


def last_kernel(flags_ref, mine_ref, theirs_ref, shift_ref, pair_ref, their_pair_ref, out_ref):
    row = lax.broadcasted_iota(jnp.int32, (ROWS, ROWS), 0)
    column = lax.broadcasted_iota(jnp.int32, (ROWS, ROWS), 1)

    def item(k, i):
        mine = mine_ref[:, i].reshape(ROWS, ROWS)
        theirs = theirs_ref[:, i].reshape(ROWS, ROWS)
        return jnp.where(flags_ref[2] == k, mine, theirs)

    def own(k):
        add = (row == column) & (flags_ref[k] == 1)
        return item(k, 0) + jnp.where(add, shift_ref[...], 0.0)

    def first(i):
        return jnp.where(flags_ref[2] == 1, pair_ref[i], their_pair_ref[i])

    inverse = first(0)
    remote = exact(inverse, item(0, 1), ((1,), (0,)))
    second = inverse_factor(first(1) - exact(remote, remote, ((0,), (0,))))
    zero = exact(inverse, own(0), ((1,), (0,)))
    rest = own(1) - exact(remote, zero, ((0,), (0,)))
    out_ref[:, :ROWS] = zero.T
    out_ref[:, ROWS:] = exact(second, rest, ((1,), (0,))).T


def last_factor(flags, mine, theirs, shift, pair, their_pair):
    return pl.pallas_call(
        last_kernel,
        out_shape=jax.ShapeDtypeStruct((ROWS, 2 * ROWS), jnp.float32),
        in_specs=[SMEM] + [VMEM] * 5,
        out_specs=VMEM,
        compiler_params=pltpu.CompilerParams(vmem_limit_bytes=16 << 20),
        cost_estimate=pl.CostEstimate(flops=64 << 20, bytes_accessed=1 << 20, transcendentals=0),
    )(flags, mine, theirs, shift, pair, their_pair)


def flip(block, bit):
    return lax.ppermute(block, "par", [(i, i ^ bit) for i in range(PAR)])


def per_device(samples, shift, panel_ids):
    here = lax.axis_index("samp")
    place = lax.axis_index("par")
    core = lax.rem(place, 2)
    chip = lax.div(place, 2)
    mine = jnp.where(core == 0, panel_ids[0], panel_ids[1])
    theirs = jnp.where(core == 0, panel_ids[1], panel_ids[0])
    axes = ("samp", "par")

    pieces = lax.all_to_all(cut(samples), "samp", 0, 0, tiled=True)

    square = lax.dot_general(
        samples, samples, (((1,), (1,)), ((), ())), preferred_element_type=jnp.float32
    )
    for bit in (1, 16, 2, 4, 8):
        square = square + flip(square, bit)
    square = square + jnp.eye(ROWS, dtype=jnp.float32) * shift[:, None]
    strip = lax.dynamic_slice_in_dim(square, chip * TILE, TILE, 0)
    pieces, strip = lax.optimization_barrier((pieces, strip))

    sent = flip(partial_gram(theirs, pieces), 1)
    total = join(core, partial_gram(mine, pieces), sent, strip)

    total = lax.all_to_all(total, axes, 0, 0, axis_index_groups=CHIPS_THEN_SAMP, tiled=True)
    strips = total[:, SAMP]
    total = total[:, :SAMP].sum(0)

    def pick(array, k):
        return lax.dynamic_index_in_dim(array, panel_ids[k], 0, keepdims=False)

    one = jnp.where(core == 0, pick(total, 1), pick(strips, 0))
    two = pick(strips, 1)
    total = jnp.stack([total, jnp.broadcast_to(one, total.shape), jnp.broadcast_to(two, total.shape)], 1)
    total = lax.all_to_all(total, axes, 0, 0, axis_index_groups=SAMP_THEN_CHIPS, tiled=True)
    blocks = total[:, 1:]
    total = total[:, :2].sum(0)

    copies = jnp.broadcast_to(total[None], (CHIPS,) + total.shape)
    gathered = lax.all_to_all(copies, "par", 0, 0, axis_index_groups=CHIPS_BY_CORE, tiled=True)
    pair = first_factor(blocks)
    their_pair = flip(pair, 1)
    gathered, pair, their_pair = lax.optimization_barrier((gathered, pair, their_pair))
    flags = jnp.stack([
        (panel_ids[0] == here).astype(jnp.int32), (panel_ids[1] == here).astype(jnp.int32), core
    ])
    return last_factor(flags, gathered, flip(gathered, 1), shift[None, :], pair, their_pair)


def solution(mesh):
    placed = (P("samp", "par"), P("samp"), P())
    return jax.shard_map(
        per_device, mesh=mesh, in_specs=placed, out_specs=P("samp", None), check_vma=False
    )
```

```python
import jax
import jax.numpy as jnp
from jax import lax
from jax.experimental import pallas as pl
from jax.experimental.pallas import tpu as pltpu
from jax.sharding import PartitionSpec as P

ROWS = 128
SAMP = 16
PAR = 32
CHIPS = PAR // 2
TILE = 8
TILES = ROWS // TILE
HIGHEST = lax.Precision.HIGHEST

OVER_CHIPS = [[[s * PAR + 2 * x + c for x in range(CHIPS)] for s in range(SAMP)] for c in range(2)]
OVER_SAMP = [[[s * PAR + 2 * x + c for s in range(SAMP)] for x in range(CHIPS)] for c in range(2)]
CHIPS_THEN_SAMP = OVER_CHIPS[0] + OVER_SAMP[1]
SAMP_THEN_CHIPS = OVER_SAMP[0] + OVER_CHIPS[1]
CHIPS_BY_CORE = [[2 * x + c for x in range(CHIPS)] for c in range(2)]


def exact(left, right, contract):
    return lax.dot_general(
        left, right, (contract, ((), ())),
        precision=HIGHEST, preferred_element_type=jnp.float32,
    )


def inverse_factor(matrix):
    lane = lax.broadcasted_iota(jnp.int32, (TILE, ROWS), 1)
    sub = lax.broadcasted_iota(jnp.int32, (TILE, ROWS), 0)
    lanes = lane[:1]
    tiles = [matrix[t * TILE:(t + 1) * TILE] for t in range(TILES)]
    for at in range(TILES):
        base = at * TILE
        rows = [tiles[at][r:r + 1] for r in range(TILE)]
        pivot = [
            [jnp.broadcast_to(rows[r][:, base + c:base + c + 1], (1, ROWS)) if c >= r else None for c in range(TILE)]
            for r in range(TILE)
        ]
        inverse = [None] * TILE
        for k in range(TILE):
            inverse[k] = 1.0 / pivot[k][k]
            scaled = jnp.where(lanes == base + k, 1.0, rows[k])
            for i in range(k + 1, TILE):
                factor = pivot[k][i] * inverse[k]
                for c in range(i, TILE):
                    pivot[i][c] = pivot[i][c] - factor * pivot[k][c]
                rows[i] = jnp.where(lanes == base + k, 0.0, rows[i]) - factor * scaled
        solved = [None] * TILE
        for k in reversed(range(TILE)):
            value = jnp.where(lanes == base + k, 1.0, rows[k])
            value = jnp.where((lanes > base + k) & (lanes < base + TILE), 0.0, value)
            for c in range(TILE - 1, k, -1):
                value = value - pivot[k][c] * solved[c]
            solved[k] = value * inverse[k]
        wide = [jnp.broadcast_to(row, (TILE, ROWS)) for row in solved]
        inside = (lane >= base) & (lane < base + TILE)
        for t in range(at + 1, TILES):
            value = jnp.where(inside, 0.0, tiles[t])
            for k in reversed(range(TILE)):
                value = value - tiles[t][:, base + k:base + k + 1] * wide[k]
            tiles[t] = value
        done = None
        for r in range(TILE):
            row = jnp.where(lanes < base + r, rows[r], jnp.where(lanes == base + r, 1.0, 0.0))
            row = jnp.broadcast_to(row * lax.rsqrt(pivot[r][r]), (TILE, ROWS))
            done = row if done is None else jnp.where(sub == r, row, done)
        tiles[at] = done
    return jnp.concatenate(tiles, 0)


def cut_kernel(samples_ref, pieces_ref, held, arrived, left):
    width = pieces_ref.shape[2]
    into = [
        pltpu.make_async_copy(samples_ref.at[:, s * width:(s + 1) * width], held.at[s], arrived.at[s])
        for s in range(SAMP)
    ]
    out = [pltpu.make_async_copy(held.at[s], pieces_ref.at[s], left.at[s]) for s in range(SAMP)]
    for copy in into:
        copy.start()
    for s in range(SAMP):
        into[s].wait()
        out[s].start()
    for copy in out:
        copy.wait()


def cut(samples):
    shape = (SAMP, ROWS, samples.shape[1] // SAMP)
    return pl.pallas_call(
        cut_kernel,
        out_shape=jax.ShapeDtypeStruct(shape, samples.dtype),
        in_specs=[pl.BlockSpec(memory_space=pl.ANY)],
        out_specs=pl.BlockSpec(memory_space=pl.ANY),
        scratch_shapes=[
            pltpu.VMEM(shape, samples.dtype),
            pltpu.SemaphoreType.DMA((SAMP,)),
            pltpu.SemaphoreType.DMA((SAMP,)),
        ],
        cost_estimate=pl.CostEstimate(flops=0, bytes_accessed=4 << 20, transcendentals=0),
    )(samples)


def gram_kernel(panel_ref, pieces_ref, total_ref):
    panel = pieces_ref[panel_ref[0]]
    for block in range(SAMP):
        total_ref[:, block] = lax.dot_general(
            panel, pieces_ref[block], (((1,), (1,)), ((), ())), preferred_element_type=jnp.float32
        ).reshape(TILES, TILE, ROWS)


VMEM = pl.BlockSpec(memory_space=pltpu.VMEM)
SMEM = pl.BlockSpec(memory_space=pltpu.SMEM)


def partial_gram(panel, pieces):
    return pl.pallas_call(
        gram_kernel,
        out_shape=jax.ShapeDtypeStruct((TILES, SAMP, TILE, ROWS), jnp.float32),
        in_specs=[SMEM, VMEM],
        out_specs=VMEM,
        compiler_params=pltpu.CompilerParams(vmem_limit_bytes=16 << 20),
        cost_estimate=pl.CostEstimate(flops=1 << 28, bytes_accessed=4 << 20, transcendentals=0),
    )(panel[None], pieces)


PART = 4


def join_kernel(core_ref, mine_ref, theirs_ref, strip_ref, out_ref, theirs_held, held, arrived, left):
    def arrival(part):
        tiles = pl.ds(part * PART, PART)
        return pltpu.make_async_copy(theirs_ref.at[tiles], theirs_held.at[tiles], arrived.at[part])

    def departure(tile, core):
        place = out_ref.at[tile, pl.ds(0, SAMP)] if core == 0 else out_ref.at[:, tile]
        return pltpu.make_async_copy(held.at[tile], place, left.at[tile])

    def strips():
        return pltpu.make_async_copy(held.at[TILES], out_ref.at[:, SAMP], left.at[TILES])

    def on_core(core, tiles, act):
        @pl.when(core_ref[0] == core)
        def _():
            for tile in tiles:
                act(departure(tile, core))

    for part in range(TILES // PART):
        arrival(part).start()
    held[TILES] = jnp.broadcast_to(strip_ref[...][None], (SAMP, TILE, ROWS))
    strips().start()
    for part in range(TILES // PART):
        arrival(part).wait()
        tiles = range(part * PART, part * PART + PART)
        for tile in tiles:
            held[tile] = mine_ref[tile] + theirs_held[tile]
        for core in range(2):
            on_core(core, tiles, lambda copy: copy.start())
    for core in range(2):
        on_core(core, range(TILES), lambda copy: copy.wait())
    strips().wait()


def join(core, mine, theirs, strip):
    anywhere = pl.BlockSpec(memory_space=pl.ANY)
    return pl.pallas_call(
        join_kernel,
        out_shape=jax.ShapeDtypeStruct((TILES, SAMP + 1, TILE, ROWS), jnp.float32),
        in_specs=[SMEM, VMEM, anywhere, VMEM],
        out_specs=anywhere,
        scratch_shapes=[
            pltpu.VMEM((TILES, SAMP, TILE, ROWS), jnp.float32),
            pltpu.VMEM((TILES + 1, SAMP, TILE, ROWS), jnp.float32),
            pltpu.SemaphoreType.DMA((TILES // PART,)),
            pltpu.SemaphoreType.DMA((TILES + 1,)),
        ],
        compiler_params=pltpu.CompilerParams(vmem_limit_bytes=16 << 20),
        cost_estimate=pl.CostEstimate(flops=1 << 20, bytes_accessed=4 << 20, transcendentals=0),
    )(core[None], mine, theirs, strip)


def first_kernel(core_ref, block_ref, inverse_ref):
    @pl.when(core_ref[0] == 0)
    def _():
        inverse_ref[...] = jnp.zeros_like(inverse_ref)

    @pl.when(core_ref[0] == 1)
    def _():
        inverse_ref[...] = inverse_factor(block_ref[...].reshape(ROWS, ROWS))


def first_factor(core, block):
    return pl.pallas_call(
        first_kernel,
        out_shape=jax.ShapeDtypeStruct((ROWS, ROWS), jnp.float32),
        in_specs=[SMEM, VMEM],
        out_specs=VMEM,
        compiler_params=pltpu.CompilerParams(vmem_limit_bytes=16 << 20),
        cost_estimate=pl.CostEstimate(flops=20 << 20, bytes_accessed=1 << 20, transcendentals=0),
    )(core[None], block)


def last_kernel(flags_ref, mine_ref, theirs_ref, shift_ref, inverse_ref, their_inverse_ref, out_ref):
    row = lax.broadcasted_iota(jnp.int32, (ROWS, ROWS), 0)
    column = lax.broadcasted_iota(jnp.int32, (ROWS, ROWS), 1)

    def item(k, i):
        mine = mine_ref[:, i].reshape(ROWS, ROWS)
        theirs = theirs_ref[:, i].reshape(ROWS, ROWS)
        return jnp.where(flags_ref[2] == k, mine, theirs)

    def own(k):
        add = (row == column) & (flags_ref[k] == 1)
        return item(k, 0) + jnp.where(add, shift_ref[...], 0.0)

    inverse = jnp.where(flags_ref[2] == 1, inverse_ref[...], their_inverse_ref[...])
    remote = exact(inverse, item(0, 1), ((1,), (0,)))
    second = inverse_factor(item(1, 1) - exact(remote, remote, ((0,), (0,))))
    zero = exact(inverse, own(0), ((1,), (0,)))
    rest = own(1) - exact(remote, zero, ((0,), (0,)))
    out_ref[:, :ROWS] = zero.T
    out_ref[:, ROWS:] = exact(second, rest, ((1,), (0,))).T


def last_factor(flags, mine, theirs, shift, inverse, their_inverse):
    return pl.pallas_call(
        last_kernel,
        out_shape=jax.ShapeDtypeStruct((ROWS, 2 * ROWS), jnp.float32),
        in_specs=[SMEM] + [VMEM] * 5,
        out_specs=VMEM,
        compiler_params=pltpu.CompilerParams(vmem_limit_bytes=16 << 20),
        cost_estimate=pl.CostEstimate(flops=64 << 20, bytes_accessed=1 << 20, transcendentals=0),
    )(flags, mine, theirs, shift, inverse, their_inverse)


def flip(block, bit):
    return lax.ppermute(block, "par", [(i, i ^ bit) for i in range(PAR)])


def per_device(samples, shift, panel_ids):
    here = lax.axis_index("samp")
    place = lax.axis_index("par")
    core = lax.rem(place, 2)
    chip = lax.div(place, 2)
    mine = jnp.where(core == 0, panel_ids[0], panel_ids[1])
    theirs = jnp.where(core == 0, panel_ids[1], panel_ids[0])
    axes = ("samp", "par")

    pieces = lax.all_to_all(cut(samples), "samp", 0, 0, tiled=True)

    square = lax.dot_general(
        samples, samples, (((1,), (1,)), ((), ())), preferred_element_type=jnp.float32
    )
    for bit in (1, 16, 2, 4, 8):
        square = square + flip(square, bit)
    square = square + jnp.eye(ROWS, dtype=jnp.float32) * shift[:, None]
    strip = lax.dynamic_slice_in_dim(square, chip * TILE, TILE, 0)
    pieces, strip = lax.optimization_barrier((pieces, strip))

    sent = flip(partial_gram(theirs, pieces), 1)
    total = join(core, partial_gram(mine, pieces), sent, strip)

    total = lax.all_to_all(total, axes, 0, 0, axis_index_groups=CHIPS_THEN_SAMP, tiled=True)
    strips = total[:, SAMP]
    total = total[:, :SAMP].sum(0)

    def pick(array, k):
        return lax.dynamic_index_in_dim(array, panel_ids[k], 0, keepdims=False)

    second = jnp.where(core == 0, pick(total, 1), pick(strips, 0))
    diagonal = pick(strips, 1)
    total = jnp.stack([total, jnp.broadcast_to(second, total.shape)], 1)
    total = lax.all_to_all(total, axes, 0, 0, axis_index_groups=SAMP_THEN_CHIPS, tiled=True)
    block = total[:, 1]
    total = total.sum(0)
    total = jnp.stack([total[0], jnp.where(core == 0, total[1], diagonal)])

    copies = jnp.broadcast_to(total[None], (CHIPS,) + total.shape)
    gathered = lax.all_to_all(copies, "par", 0, 0, axis_index_groups=CHIPS_BY_CORE, tiled=True)
    inverse = first_factor(core, block)
    their_inverse = flip(inverse, 1)
    gathered, inverse, their_inverse = lax.optimization_barrier((gathered, inverse, their_inverse))
    flags = jnp.stack([
        (panel_ids[0] == here).astype(jnp.int32), (panel_ids[1] == here).astype(jnp.int32), core
    ])
    return last_factor(flags, gathered, flip(gathered, 1), shift[None, :], inverse, their_inverse)


def solution(mesh):
    placed = (P("samp", "par"), P("samp"), P())
    return jax.shard_map(
        per_device, mesh=mesh, in_specs=placed, out_specs=P("samp", None), check_vma=False
    )
```

```python
import jax
import jax.numpy as jnp
from jax import lax
from jax.experimental import pallas as pl
from jax.experimental.pallas import tpu as pltpu
from jax.sharding import PartitionSpec as P

ROWS = 128
SAMP = 16
PAR = 32
CHIPS = PAR // 2
TILE = 8
TILES = ROWS // TILE
HIGHEST = lax.Precision.HIGHEST

OVER_CHIPS = [[[s * PAR + 2 * x + c for x in range(CHIPS)] for s in range(SAMP)] for c in range(2)]
OVER_SAMP = [[[s * PAR + 2 * x + c for s in range(SAMP)] for x in range(CHIPS)] for c in range(2)]
CHIPS_THEN_SAMP = OVER_CHIPS[1] + OVER_SAMP[0]
SAMP_THEN_CHIPS = OVER_SAMP[1] + OVER_CHIPS[0]
CHIPS_BY_CORE = [[2 * x + c for x in range(CHIPS)] for c in range(2)]


def exact(left, right, contract):
    return lax.dot_general(
        left, right, (contract, ((), ())),
        precision=HIGHEST, preferred_element_type=jnp.float32,
    )


def inverse_factor(matrix):
    lane = lax.broadcasted_iota(jnp.int32, (TILE, ROWS), 1)
    sub = lax.broadcasted_iota(jnp.int32, (TILE, ROWS), 0)
    lanes = lane[:1]
    tiles = [matrix[t * TILE:(t + 1) * TILE] for t in range(TILES)]
    for at in range(TILES):
        base = at * TILE
        rows = [tiles[at][r:r + 1] for r in range(TILE)]
        pivot = [
            [jnp.broadcast_to(rows[r][:, base + c:base + c + 1], (1, ROWS)) if c >= r else None for c in range(TILE)]
            for r in range(TILE)
        ]
        inside = (lane >= base) & (lane < base + TILE)
        near = at + 1 < TILES
        if near:
            after = jnp.where(inside, 0.0, tiles[at + 1])
            columns = [
                jnp.broadcast_to(tiles[at + 1][:, base + k:base + k + 1], (TILE, ROWS)) for k in range(TILE)
            ]
        inverse = [None] * TILE
        for k in range(TILE):
            inverse[k] = 1.0 / pivot[k][k]
            scaled = jnp.where(lanes == base + k, 1.0, rows[k])
            factors = [None] * TILE
            for i in range(k + 1, TILE):
                factors[i] = pivot[k][i] * inverse[k]
                for c in range(i, TILE):
                    pivot[i][c] = pivot[i][c] - factors[i] * pivot[k][c]
                rows[i] = jnp.where(lanes == base + k, 0.0, rows[i]) - factors[i] * scaled
            if near:
                lower = jnp.where((lanes > base + k) & (lanes < base + TILE), 0.0, scaled) * inverse[k]
                after = after - columns[k] * lower
                for i in range(k + 1, TILE):
                    columns[i] = columns[i] - factors[i] * columns[k]
        if at + 2 < TILES:
            solved = [None] * TILE
            for k in reversed(range(TILE)):
                value = jnp.where(lanes == base + k, 1.0, rows[k])
                value = jnp.where((lanes > base + k) & (lanes < base + TILE), 0.0, value)
                for c in range(TILE - 1, k, -1):
                    value = value - pivot[k][c] * solved[c]
                solved[k] = value * inverse[k]
            wide = [jnp.broadcast_to(row, (TILE, ROWS)) for row in solved]
        for t in range(at + 2, TILES):
            value = jnp.where(inside, 0.0, tiles[t])
            for k in reversed(range(TILE)):
                value = value - tiles[t][:, base + k:base + k + 1] * wide[k]
            tiles[t] = value
        if near:
            tiles[at + 1] = after
        done = None
        for r in range(TILE):
            row = jnp.where(lanes < base + r, rows[r], jnp.where(lanes == base + r, 1.0, 0.0))
            row = jnp.broadcast_to(row * lax.rsqrt(pivot[r][r]), (TILE, ROWS))
            done = row if done is None else jnp.where(sub == r, row, done)
        tiles[at] = done
    return jnp.concatenate(tiles, 0)


def cut_kernel(samples_ref, pieces_ref, held, arrived, left):
    width = pieces_ref.shape[2]
    into = [
        pltpu.make_async_copy(samples_ref.at[:, s * width:(s + 1) * width], held.at[s], arrived.at[s])
        for s in range(SAMP)
    ]
    out = [pltpu.make_async_copy(held.at[s], pieces_ref.at[s], left.at[s]) for s in range(SAMP)]
    for copy in into:
        copy.start()
    for s in range(SAMP):
        into[s].wait()
        out[s].start()
    for copy in out:
        copy.wait()


def cut(samples):
    shape = (SAMP, ROWS, samples.shape[1] // SAMP)
    return pl.pallas_call(
        cut_kernel,
        out_shape=jax.ShapeDtypeStruct(shape, samples.dtype),
        in_specs=[pl.BlockSpec(memory_space=pl.ANY)],
        out_specs=pl.BlockSpec(memory_space=pl.ANY),
        scratch_shapes=[
            pltpu.VMEM(shape, samples.dtype),
            pltpu.SemaphoreType.DMA((SAMP,)),
            pltpu.SemaphoreType.DMA((SAMP,)),
        ],
        cost_estimate=pl.CostEstimate(flops=0, bytes_accessed=4 << 20, transcendentals=0),
    )(samples)


def gram_kernel(panel_ref, pieces_ref, total_ref):
    panel = pieces_ref[panel_ref[0]]
    for block in range(SAMP):
        total_ref[:, block] = lax.dot_general(
            panel, pieces_ref[block], (((1,), (1,)), ((), ())), preferred_element_type=jnp.float32
        ).reshape(TILES, TILE, ROWS)


VMEM = pl.BlockSpec(memory_space=pltpu.VMEM)
SMEM = pl.BlockSpec(memory_space=pltpu.SMEM)


def partial_gram(panel, pieces):
    return pl.pallas_call(
        gram_kernel,
        out_shape=jax.ShapeDtypeStruct((TILES, SAMP, TILE, ROWS), jnp.float32),
        in_specs=[SMEM, VMEM],
        out_specs=VMEM,
        compiler_params=pltpu.CompilerParams(vmem_limit_bytes=16 << 20),
        cost_estimate=pl.CostEstimate(flops=1 << 28, bytes_accessed=4 << 20, transcendentals=0),
    )(panel[None], pieces)


PART = 4


def join_kernel(role_ref, mine_ref, theirs_ref, strip_ref, out_ref, theirs_held, held, arrived, left):
    def arrival(part):
        tiles = pl.ds(part * PART, PART)
        return pltpu.make_async_copy(theirs_ref.at[tiles], theirs_held.at[tiles], arrived.at[part])

    def departure(tile, core):
        place = out_ref.at[tile, pl.ds(0, SAMP)] if core == 0 else out_ref.at[:, tile]
        return pltpu.make_async_copy(held.at[tile], place, left.at[tile])

    def strips():
        return pltpu.make_async_copy(held.at[TILES], out_ref.at[:, SAMP], left.at[TILES])

    def on_core(core, tiles, act):
        @pl.when(role_ref[0] == core)
        def _():
            for tile in tiles:
                act(departure(tile, core))

    for part in range(TILES // PART):
        arrival(part).start()
    held[TILES] = jnp.broadcast_to(strip_ref[...][None], (SAMP, TILE, ROWS))
    strips().start()
    for part in range(TILES // PART):
        arrival(part).wait()
        tiles = range(part * PART, part * PART + PART)
        for tile in tiles:
            held[tile] = mine_ref[tile] + theirs_held[tile]
        for core in range(2):
            on_core(core, tiles, lambda copy: copy.start())
    for core in range(2):
        on_core(core, range(TILES), lambda copy: copy.wait())
    strips().wait()


def join(role, mine, theirs, strip):
    anywhere = pl.BlockSpec(memory_space=pl.ANY)
    return pl.pallas_call(
        join_kernel,
        out_shape=jax.ShapeDtypeStruct((TILES, SAMP + 1, TILE, ROWS), jnp.float32),
        in_specs=[SMEM, VMEM, anywhere, VMEM],
        out_specs=anywhere,
        scratch_shapes=[
            pltpu.VMEM((TILES, SAMP, TILE, ROWS), jnp.float32),
            pltpu.VMEM((TILES + 1, SAMP, TILE, ROWS), jnp.float32),
            pltpu.SemaphoreType.DMA((TILES // PART,)),
            pltpu.SemaphoreType.DMA((TILES + 1,)),
        ],
        compiler_params=pltpu.CompilerParams(vmem_limit_bytes=16 << 20),
        cost_estimate=pl.CostEstimate(flops=1 << 20, bytes_accessed=4 << 20, transcendentals=0),
    )(role[None], mine, theirs, strip)


def first_kernel(role_ref, block_ref, inverse_ref):
    @pl.when(role_ref[0] == 0)
    def _():
        inverse_ref[...] = jnp.zeros_like(inverse_ref)

    @pl.when(role_ref[0] == 1)
    def _():
        inverse_ref[...] = inverse_factor(block_ref[...].reshape(ROWS, ROWS))


def first_factor(role, block):
    return pl.pallas_call(
        first_kernel,
        out_shape=jax.ShapeDtypeStruct((ROWS, ROWS), jnp.float32),
        in_specs=[SMEM, VMEM],
        out_specs=VMEM,
        compiler_params=pltpu.CompilerParams(vmem_limit_bytes=16 << 20),
        cost_estimate=pl.CostEstimate(flops=20 << 20, bytes_accessed=1 << 20, transcendentals=0),
    )(role[None], block)


def last_kernel(flags_ref, mine_ref, theirs_ref, shift_ref, inverse_ref, their_inverse_ref, out_ref):
    row = lax.broadcasted_iota(jnp.int32, (ROWS, ROWS), 0)
    column = lax.broadcasted_iota(jnp.int32, (ROWS, ROWS), 1)

    def item(k, i):
        mine = mine_ref[:, i].reshape(ROWS, ROWS)
        theirs = theirs_ref[:, i].reshape(ROWS, ROWS)
        return jnp.where(flags_ref[2] == k, mine, theirs)

    def own(k):
        add = (row == column) & (flags_ref[k] == 1)
        return item(k, 0) + jnp.where(add, shift_ref[...], 0.0)

    inverse = jnp.where(flags_ref[2] == 1, inverse_ref[...], their_inverse_ref[...])
    remote = exact(inverse, item(0, 1), ((1,), (0,)))
    second = inverse_factor(item(1, 1) - exact(remote, remote, ((0,), (0,))))
    zero = exact(inverse, own(0), ((1,), (0,)))
    rest = own(1) - exact(remote, zero, ((0,), (0,)))
    out_ref[:, :ROWS] = zero.T
    out_ref[:, ROWS:] = exact(second, rest, ((1,), (0,))).T


def last_factor(flags, mine, theirs, shift, inverse, their_inverse):
    return pl.pallas_call(
        last_kernel,
        out_shape=jax.ShapeDtypeStruct((ROWS, 2 * ROWS), jnp.float32),
        in_specs=[SMEM] + [VMEM] * 5,
        out_specs=VMEM,
        compiler_params=pltpu.CompilerParams(vmem_limit_bytes=16 << 20),
        cost_estimate=pl.CostEstimate(flops=64 << 20, bytes_accessed=1 << 20, transcendentals=0),
    )(flags, mine, theirs, shift, inverse, their_inverse)


def flip(block, bit):
    return lax.ppermute(block, "par", [(i, i ^ bit) for i in range(PAR)])


def per_device(samples, shift, panel_ids):
    here = lax.axis_index("samp")
    place = lax.axis_index("par")
    role = 1 - lax.rem(place, 2)
    chip = lax.div(place, 2)
    mine = jnp.where(role == 0, panel_ids[0], panel_ids[1])
    theirs = jnp.where(role == 0, panel_ids[1], panel_ids[0])
    axes = ("samp", "par")

    pieces = lax.all_to_all(cut(samples), "samp", 0, 0, tiled=True)

    square = lax.dot_general(
        samples, samples, (((1,), (1,)), ((), ())), preferred_element_type=jnp.float32
    )
    for bit in (1, 16, 2, 4, 8):
        square = square + flip(square, bit)
    square = square + jnp.eye(ROWS, dtype=jnp.float32) * shift[:, None]
    strip = lax.dynamic_slice_in_dim(square, chip * TILE, TILE, 0)
    pieces, strip = lax.optimization_barrier((pieces, strip))

    sent = flip(partial_gram(theirs, pieces), 1)
    total = join(role, partial_gram(mine, pieces), sent, strip)

    total = lax.all_to_all(total, axes, 0, 0, axis_index_groups=CHIPS_THEN_SAMP, tiled=True)
    strips = total[:, SAMP]
    total = total[:, :SAMP].sum(0)

    def pick(array, k):
        return lax.dynamic_index_in_dim(array, panel_ids[k], 0, keepdims=False)

    second = jnp.where(role == 0, pick(total, 1), pick(strips, 0))
    diagonal = pick(strips, 1)
    total = jnp.stack([total, jnp.broadcast_to(second, total.shape)], 1)
    total = lax.all_to_all(total, axes, 0, 0, axis_index_groups=SAMP_THEN_CHIPS, tiled=True)
    block = total[:, 1]
    total = total.sum(0)
    total = jnp.stack([total[0], jnp.where(role == 0, total[1], diagonal)])

    copies = jnp.broadcast_to(total[None], (CHIPS,) + total.shape)
    gathered = lax.all_to_all(copies, "par", 0, 0, axis_index_groups=CHIPS_BY_CORE, tiled=True)
    inverse = first_factor(role, block)
    their_inverse = flip(inverse, 1)
    gathered, inverse, their_inverse = lax.optimization_barrier((gathered, inverse, their_inverse))
    flags = jnp.stack([
        (panel_ids[0] == here).astype(jnp.int32), (panel_ids[1] == here).astype(jnp.int32), role
    ])
    return last_factor(flags, gathered, flip(gathered, 1), shift[None, :], inverse, their_inverse)


def solution(mesh):
    placed = (P("samp", "par"), P("samp"), P())
    return jax.shard_map(
        per_device, mesh=mesh, in_specs=placed, out_specs=P("samp", None), check_vma=False
    )
```

```python
import jax
import jax.numpy as jnp
from jax import lax
from jax.experimental import pallas as pl
from jax.experimental.pallas import tpu as pltpu
from jax.sharding import PartitionSpec as P

ROWS = 128
SAMP = 16
PAR = 32
CHIPS = PAR // 2
TILE = 8
TILES = ROWS // TILE
HIGHEST = lax.Precision.HIGHEST

OVER_CHIPS = [[[s * PAR + 2 * x + c for x in range(CHIPS)] for s in range(SAMP)] for c in range(2)]
OVER_SAMP = [[[s * PAR + 2 * x + c for s in range(SAMP)] for x in range(CHIPS)] for c in range(2)]
CHIPS_THEN_SAMP = OVER_CHIPS[1] + OVER_SAMP[0]
SAMP_THEN_CHIPS = OVER_SAMP[1] + OVER_CHIPS[0]
CHIPS_BY_CORE = [[2 * x + c for x in range(CHIPS)] for c in range(2)]


def exact(left, right, contract):
    return lax.dot_general(
        left, right, (contract, ((), ())),
        precision=HIGHEST, preferred_element_type=jnp.float32,
    )


def inverse_factor(matrix):
    lane = lax.broadcasted_iota(jnp.int32, (TILE, ROWS), 1)
    sub = lax.broadcasted_iota(jnp.int32, (TILE, ROWS), 0)
    lanes = lane[:1]
    tiles = [matrix[t * TILE:(t + 1) * TILE] for t in range(TILES)]
    for at in range(TILES):
        base = at * TILE
        rows = [tiles[at][r:r + 1] for r in range(TILE)]
        pivot = [
            [jnp.broadcast_to(rows[r][:, base + c:base + c + 1], (1, ROWS)) if c >= r else None for c in range(TILE)]
            for r in range(TILE)
        ]
        inside = (lane >= base) & (lane < base + TILE)
        near = at + 1 < TILES
        if near:
            after = jnp.where(inside, 0.0, tiles[at + 1])
            columns = [
                jnp.broadcast_to(tiles[at + 1][:, base + k:base + k + 1], (TILE, ROWS)) for k in range(TILE)
            ]
        inverse = [None] * TILE
        for k in range(TILE):
            inverse[k] = 1.0 / pivot[k][k]
            scaled = jnp.where(lanes == base + k, 1.0, rows[k])
            factors = [None] * TILE
            for i in range(k + 1, TILE):
                factors[i] = pivot[k][i] * inverse[k]
                for c in range(i, TILE):
                    pivot[i][c] = pivot[i][c] - factors[i] * pivot[k][c]
                rows[i] = jnp.where(lanes == base + k, 0.0, rows[i]) - factors[i] * scaled
            if near:
                lower = jnp.where((lanes > base + k) & (lanes < base + TILE), 0.0, scaled) * inverse[k]
                after = after - columns[k] * lower
                for i in range(k + 1, TILE):
                    columns[i] = columns[i] - factors[i] * columns[k]
        if at + 2 < TILES:
            solved = [None] * TILE
            for k in reversed(range(TILE)):
                value = jnp.where(lanes == base + k, 1.0, rows[k])
                value = jnp.where((lanes > base + k) & (lanes < base + TILE), 0.0, value)
                for c in range(TILE - 1, k, -1):
                    value = value - pivot[k][c] * solved[c]
                solved[k] = value * inverse[k]
            wide = [jnp.broadcast_to(row, (TILE, ROWS)) for row in solved]
        for t in range(at + 2, TILES):
            value = jnp.where(inside, 0.0, tiles[t])
            for k in reversed(range(TILE)):
                value = value - tiles[t][:, base + k:base + k + 1] * wide[k]
            tiles[t] = value
        if near:
            tiles[at + 1] = after
        done = None
        for r in range(TILE):
            row = jnp.where(lanes < base + r, rows[r], jnp.where(lanes == base + r, 1.0, 0.0))
            row = jnp.broadcast_to(row * lax.rsqrt(pivot[r][r]), (TILE, ROWS))
            done = row if done is None else jnp.where(sub == r, row, done)
        tiles[at] = done
    return jnp.concatenate(tiles, 0)


def cut_kernel(samples_ref, pieces_ref, held, arrived, left):
    width = pieces_ref.shape[2]
    into = [
        pltpu.make_async_copy(samples_ref.at[:, s * width:(s + 1) * width], held.at[s], arrived.at[s])
        for s in range(SAMP)
    ]
    out = [pltpu.make_async_copy(held.at[s], pieces_ref.at[s], left.at[s]) for s in range(SAMP)]
    for copy in into:
        copy.start()
    for s in range(SAMP):
        into[s].wait()
        out[s].start()
    for copy in out:
        copy.wait()


def cut(samples):
    shape = (SAMP, ROWS, samples.shape[1] // SAMP)
    return pl.pallas_call(
        cut_kernel,
        out_shape=jax.ShapeDtypeStruct(shape, samples.dtype),
        in_specs=[pl.BlockSpec(memory_space=pl.ANY)],
        out_specs=pl.BlockSpec(memory_space=pl.ANY),
        scratch_shapes=[
            pltpu.VMEM(shape, samples.dtype),
            pltpu.SemaphoreType.DMA((SAMP,)),
            pltpu.SemaphoreType.DMA((SAMP,)),
        ],
        cost_estimate=pl.CostEstimate(flops=0, bytes_accessed=4 << 20, transcendentals=0),
    )(samples)


def gram_kernel(panel_ref, pieces_ref, total_ref):
    panel = pieces_ref[panel_ref[0]]
    for block in range(SAMP):
        total_ref[:, block] = lax.dot_general(
            panel, pieces_ref[block], (((1,), (1,)), ((), ())), preferred_element_type=jnp.float32
        ).reshape(TILES, TILE, ROWS)


VMEM = pl.BlockSpec(memory_space=pltpu.VMEM)
SMEM = pl.BlockSpec(memory_space=pltpu.SMEM)


def partial_gram(panel, pieces):
    return pl.pallas_call(
        gram_kernel,
        out_shape=jax.ShapeDtypeStruct((TILES, SAMP, TILE, ROWS), jnp.float32),
        in_specs=[SMEM, VMEM],
        out_specs=VMEM,
        compiler_params=pltpu.CompilerParams(vmem_limit_bytes=16 << 20),
        cost_estimate=pl.CostEstimate(flops=1 << 28, bytes_accessed=4 << 20, transcendentals=0),
    )(panel, pieces)


def join_kernel(role_ref, mine_ref, theirs_ref, strip_ref, out_ref, held, left):
    def departure(tile, role):
        place = out_ref.at[tile, pl.ds(0, SAMP)] if role == 0 else out_ref.at[:, tile]
        return pltpu.make_async_copy(held.at[tile], place, left.at[tile])

    def strips():
        return pltpu.make_async_copy(held.at[TILES], out_ref.at[:, SAMP], left.at[TILES])

    def in_role(role, tiles, act):
        @pl.when(role_ref[0] == role)
        def _():
            for tile in tiles:
                act(departure(tile, role))

    held[TILES] = jnp.broadcast_to(strip_ref[...][None], (SAMP, TILE, ROWS))
    strips().start()
    for tile in range(TILES):
        held[tile] = mine_ref[tile] + theirs_ref[tile]
        for role in range(2):
            in_role(role, [tile], lambda copy: copy.start())
    for role in range(2):
        in_role(role, range(TILES), lambda copy: copy.wait())
    strips().wait()


def join(role, mine, theirs, strip):
    return pl.pallas_call(
        join_kernel,
        out_shape=jax.ShapeDtypeStruct((TILES, SAMP + 1, TILE, ROWS), jnp.float32),
        in_specs=[SMEM, VMEM, VMEM, VMEM],
        out_specs=pl.BlockSpec(memory_space=pl.ANY),
        scratch_shapes=[
            pltpu.VMEM((TILES + 1, SAMP, TILE, ROWS), jnp.float32),
            pltpu.SemaphoreType.DMA((TILES + 1,)),
        ],
        compiler_params=pltpu.CompilerParams(vmem_limit_bytes=16 << 20),
        cost_estimate=pl.CostEstimate(flops=1 << 20, bytes_accessed=4 << 20, transcendentals=0),
    )(role[None], mine, theirs, strip)


def first_kernel(role_ref, block_ref, inverse_ref):
    @pl.when(role_ref[0] == 0)
    def _():
        inverse_ref[...] = jnp.zeros_like(inverse_ref)

    @pl.when(role_ref[0] == 1)
    def _():
        inverse_ref[...] = inverse_factor(block_ref[...].reshape(ROWS, ROWS))


def first_factor(role, block):
    return pl.pallas_call(
        first_kernel,
        out_shape=jax.ShapeDtypeStruct((ROWS, ROWS), jnp.float32),
        in_specs=[SMEM, VMEM],
        out_specs=VMEM,
        compiler_params=pltpu.CompilerParams(vmem_limit_bytes=16 << 20),
        cost_estimate=pl.CostEstimate(flops=20 << 20, bytes_accessed=1 << 20, transcendentals=0),
    )(role[None], block)


def last_kernel(flags_ref, mine_ref, theirs_ref, shift_ref, inverse_ref, their_inverse_ref, out_ref):
    row = lax.broadcasted_iota(jnp.int32, (ROWS, ROWS), 0)
    column = lax.broadcasted_iota(jnp.int32, (ROWS, ROWS), 1)

    def item(k, i):
        mine = mine_ref[:, i].reshape(ROWS, ROWS)
        theirs = theirs_ref[:, i].reshape(ROWS, ROWS)
        return jnp.where(flags_ref[2] == k, mine, theirs)

    def own(k):
        add = (row == column) & (flags_ref[k] == 1)
        return item(k, 0) + jnp.where(add, shift_ref[...], 0.0)

    inverse = jnp.where(flags_ref[2] == 1, inverse_ref[...], their_inverse_ref[...])
    remote = exact(inverse, item(0, 1), ((1,), (0,)))
    second = inverse_factor(item(1, 1) - exact(remote, remote, ((0,), (0,))))
    zero = exact(inverse, own(0), ((1,), (0,)))
    rest = own(1) - exact(remote, zero, ((0,), (0,)))
    out_ref[:, :ROWS] = zero.T
    out_ref[:, ROWS:] = exact(second, rest, ((1,), (0,))).T


def last_factor(flags, mine, theirs, shift, inverse, their_inverse):
    return pl.pallas_call(
        last_kernel,
        out_shape=jax.ShapeDtypeStruct((ROWS, 2 * ROWS), jnp.float32),
        in_specs=[SMEM] + [VMEM] * 5,
        out_specs=VMEM,
        compiler_params=pltpu.CompilerParams(vmem_limit_bytes=16 << 20),
        cost_estimate=pl.CostEstimate(flops=64 << 20, bytes_accessed=1 << 20, transcendentals=0),
    )(flags, mine, theirs, shift, inverse, their_inverse)


def flip(block, bit):
    return lax.ppermute(block, "par", [(i, i ^ bit) for i in range(PAR)])


def per_device(samples, shift, panel_ids):
    here = lax.axis_index("samp")
    place = lax.axis_index("par")
    role = 1 - lax.rem(place, 2)
    chip = lax.div(place, 2)
    mine = jnp.where(role == 0, panel_ids[0], panel_ids[1])
    theirs = jnp.where(role == 0, panel_ids[1], panel_ids[0])
    axes = ("samp", "par")

    pieces = lax.all_to_all(cut(samples), "samp", 0, 0, tiled=True)

    square = lax.dot_general(
        samples, samples, (((1,), (1,)), ((), ())), preferred_element_type=jnp.float32
    )
    for bit in (1, 16, 2, 4, 8):
        square = square + flip(square, bit)
    square = square + jnp.eye(ROWS, dtype=jnp.float32) * shift[:, None]
    strip = lax.dynamic_slice_in_dim(square, chip * TILE, TILE, 0)
    flags = jnp.stack([
        (panel_ids[0] == here).astype(jnp.int32), (panel_ids[1] == here).astype(jnp.int32), role
    ])
    pieces, strip, flags, mine, theirs = lax.optimization_barrier((pieces, strip, flags, mine[None], theirs[None]))

    sent = flip(partial_gram(theirs, pieces), 1)
    total = join(role, partial_gram(mine, pieces), sent, strip)

    total = lax.all_to_all(total, axes, 0, 0, axis_index_groups=CHIPS_THEN_SAMP, tiled=True)
    strips = total[:, SAMP]
    total = total[:, :SAMP].sum(0)

    def pick(array, k):
        return lax.dynamic_index_in_dim(array, panel_ids[k], 0, keepdims=False)

    second = jnp.where(role == 0, pick(total, 1), pick(strips, 0))
    diagonal = pick(strips, 1)
    total = jnp.stack([total, jnp.broadcast_to(second, total.shape)], 1)
    total = lax.all_to_all(total, axes, 0, 0, axis_index_groups=SAMP_THEN_CHIPS, tiled=True)
    block = total[:, 1]
    total = total.sum(0)
    total = jnp.stack([total[0], jnp.where(role == 0, total[1], diagonal)])

    copies = jnp.broadcast_to(total[None], (CHIPS,) + total.shape)
    gathered = lax.all_to_all(copies, "par", 0, 0, axis_index_groups=CHIPS_BY_CORE, tiled=True)
    inverse = first_factor(role, block)
    their_inverse = flip(inverse, 1)
    gathered, inverse, their_inverse = lax.optimization_barrier((gathered, inverse, their_inverse))
    return last_factor(flags, gathered, flip(gathered, 1), shift[None, :], inverse, their_inverse)


def solution(mesh):
    placed = (P("samp", "par"), P("samp"), P())
    return jax.shard_map(
        per_device, mesh=mesh, in_specs=placed, out_specs=P("samp", None), check_vma=False
    )
```

```python
import jax
import jax.numpy as jnp
from jax import lax
from jax.experimental import pallas as pl
from jax.experimental.pallas import tpu as pltpu
from jax.sharding import PartitionSpec as P

ROWS = 128
SAMP = 16
PAR = 32
CHIPS = PAR // 2
TILE = 8
TILES = ROWS // TILE
HIGHEST = lax.Precision.HIGHEST

OVER_CHIPS = [[[s * PAR + 2 * x + c for x in range(CHIPS)] for s in range(SAMP)] for c in range(2)]
OVER_SAMP = [[[s * PAR + 2 * x + c for s in range(SAMP)] for x in range(CHIPS)] for c in range(2)]
CHIPS_THEN_SAMP = OVER_CHIPS[1] + OVER_SAMP[0]
SAMP_THEN_CHIPS = OVER_SAMP[1] + OVER_CHIPS[0]
CHIPS_BY_CORE = [[2 * x + c for x in range(CHIPS)] for c in range(2)]


def exact(left, right, contract):
    return lax.dot_general(
        left, right, (contract, ((), ())),
        precision=HIGHEST, preferred_element_type=jnp.float32,
    )


def inverse_factor(matrix):
    lane = lax.broadcasted_iota(jnp.int32, (TILE, ROWS), 1)
    sub = lax.broadcasted_iota(jnp.int32, (TILE, ROWS), 0)
    lanes = lane[:1]
    tiles = [matrix[t * TILE:(t + 1) * TILE] for t in range(TILES)]
    for at in range(TILES):
        base = at * TILE
        rows = [tiles[at][r:r + 1] for r in range(TILE)]
        pivot = [
            [jnp.broadcast_to(rows[r][:, base + c:base + c + 1], (1, ROWS)) if c >= r else None for c in range(TILE)]
            for r in range(TILE)
        ]
        inside = (lane >= base) & (lane < base + TILE)
        near = at + 1 < TILES
        if near:
            after = jnp.where(inside, 0.0, tiles[at + 1])
            columns = [
                jnp.broadcast_to(tiles[at + 1][:, base + k:base + k + 1], (TILE, ROWS)) for k in range(TILE)
            ]
        inverse = [None] * TILE
        for k in range(TILE):
            inverse[k] = 1.0 / pivot[k][k]
            scaled = jnp.where(lanes == base + k, 1.0, rows[k])
            factors = [None] * TILE
            for i in range(k + 1, TILE):
                factors[i] = pivot[k][i] * inverse[k]
                for c in range(i, TILE):
                    pivot[i][c] = pivot[i][c] - factors[i] * pivot[k][c]
                rows[i] = jnp.where(lanes == base + k, 0.0, rows[i]) - factors[i] * scaled
            if near:
                lower = jnp.where((lanes > base + k) & (lanes < base + TILE), 0.0, scaled) * inverse[k]
                after = after - columns[k] * lower
                for i in range(k + 1, TILE):
                    columns[i] = columns[i] - factors[i] * columns[k]
        if at + 2 < TILES:
            solved = [None] * TILE
            for k in reversed(range(TILE)):
                value = jnp.where(lanes == base + k, 1.0, rows[k])
                value = jnp.where((lanes > base + k) & (lanes < base + TILE), 0.0, value)
                for c in range(TILE - 1, k, -1):
                    value = value - pivot[k][c] * solved[c]
                solved[k] = value * inverse[k]
            wide = [jnp.broadcast_to(row, (TILE, ROWS)) for row in solved]
        for t in range(at + 2, TILES):
            value = jnp.where(inside, 0.0, tiles[t])
            for k in reversed(range(TILE)):
                value = value - tiles[t][:, base + k:base + k + 1] * wide[k]
            tiles[t] = value
        if near:
            tiles[at + 1] = after
        done = None
        for r in range(TILE):
            row = jnp.where(lanes < base + r, rows[r], jnp.where(lanes == base + r, 1.0, 0.0))
            row = jnp.broadcast_to(row * lax.rsqrt(pivot[r][r]), (TILE, ROWS))
            done = row if done is None else jnp.where(sub == r, row, done)
        tiles[at] = done
    return jnp.concatenate(tiles, 0)


def cut_kernel(samples_ref, pieces_ref, held, arrived, left):
    width = pieces_ref.shape[2]
    into = [
        pltpu.make_async_copy(samples_ref.at[:, s * width:(s + 1) * width], held.at[s], arrived.at[s])
        for s in range(SAMP)
    ]
    out = [pltpu.make_async_copy(held.at[s], pieces_ref.at[s], left.at[s]) for s in range(SAMP)]
    for copy in into:
        copy.start()
    for s in range(SAMP):
        into[s].wait()
        out[s].start()
    for copy in out:
        copy.wait()


def cut(samples):
    shape = (SAMP, ROWS, samples.shape[1] // SAMP)
    return pl.pallas_call(
        cut_kernel,
        out_shape=jax.ShapeDtypeStruct(shape, samples.dtype),
        in_specs=[pl.BlockSpec(memory_space=pl.ANY)],
        out_specs=pl.BlockSpec(memory_space=pl.ANY),
        scratch_shapes=[
            pltpu.VMEM(shape, samples.dtype),
            pltpu.SemaphoreType.DMA((SAMP,)),
            pltpu.SemaphoreType.DMA((SAMP,)),
        ],
        cost_estimate=pl.CostEstimate(flops=0, bytes_accessed=4 << 20, transcendentals=0),
    )(samples)


def gram_kernel(panel_ref, pieces_ref, total_ref):
    panel = pieces_ref[panel_ref[0]]
    for block in range(SAMP):
        total_ref[:, block] = lax.dot_general(
            panel, pieces_ref[block], (((1,), (1,)), ((), ())), preferred_element_type=jnp.float32
        ).reshape(TILES, TILE, ROWS)


VMEM = pl.BlockSpec(memory_space=pltpu.VMEM)
SMEM = pl.BlockSpec(memory_space=pltpu.SMEM)


def partial_gram(panel, pieces):
    return pl.pallas_call(
        gram_kernel,
        out_shape=jax.ShapeDtypeStruct((TILES, SAMP, TILE, ROWS), jnp.float32),
        in_specs=[SMEM, VMEM],
        out_specs=VMEM,
        compiler_params=pltpu.CompilerParams(vmem_limit_bytes=16 << 20),
        cost_estimate=pl.CostEstimate(flops=1 << 28, bytes_accessed=4 << 20, transcendentals=0),
    )(panel, pieces)


def join_kernel(role_ref, mine_ref, theirs_ref, strip_ref, out_ref, held, left):
    def departure(tile, role):
        place = out_ref.at[tile, pl.ds(0, SAMP)] if role == 0 else out_ref.at[:, tile]
        return pltpu.make_async_copy(held.at[tile], place, left.at[tile])

    def strips():
        return pltpu.make_async_copy(held.at[TILES], out_ref.at[:, SAMP], left.at[TILES])

    def send(role):
        @pl.when(role_ref[0] == role)
        def _():
            for tile in range(TILES):
                held[tile] = mine_ref[tile] + theirs_ref[tile]
                departure(tile, role).start()
            for tile in range(TILES):
                departure(tile, role).wait()

    held[TILES] = jnp.broadcast_to(strip_ref[...][None], (SAMP, TILE, ROWS))
    strips().start()
    send(0)
    send(1)
    strips().wait()


def join(role, mine, theirs, strip):
    return pl.pallas_call(
        join_kernel,
        out_shape=jax.ShapeDtypeStruct((TILES, SAMP + 1, TILE, ROWS), jnp.float32),
        in_specs=[SMEM, VMEM, VMEM, VMEM],
        out_specs=pl.BlockSpec(memory_space=pl.ANY),
        scratch_shapes=[
            pltpu.VMEM((TILES + 1, SAMP, TILE, ROWS), jnp.float32),
            pltpu.SemaphoreType.DMA((TILES + 1,)),
        ],
        compiler_params=pltpu.CompilerParams(vmem_limit_bytes=16 << 20),
        cost_estimate=pl.CostEstimate(flops=1 << 20, bytes_accessed=4 << 20, transcendentals=0),
    )(role[None], mine, theirs, strip)


def first_kernel(role_ref, block_ref, inverse_ref):
    @pl.when(role_ref[0] == 0)
    def _():
        inverse_ref[...] = jnp.zeros_like(inverse_ref)

    @pl.when(role_ref[0] == 1)
    def _():
        inverse_ref[...] = inverse_factor(block_ref[...].reshape(ROWS, ROWS))


def first_factor(role, block):
    return pl.pallas_call(
        first_kernel,
        out_shape=jax.ShapeDtypeStruct((ROWS, ROWS), jnp.float32),
        in_specs=[SMEM, VMEM],
        out_specs=VMEM,
        compiler_params=pltpu.CompilerParams(vmem_limit_bytes=16 << 20),
        cost_estimate=pl.CostEstimate(flops=20 << 20, bytes_accessed=1 << 20, transcendentals=0),
    )(role[None], block)


def last_kernel(flags_ref, mine_ref, theirs_ref, shift_ref, inverse_ref, their_inverse_ref, out_ref):
    row = lax.broadcasted_iota(jnp.int32, (ROWS, ROWS), 0)
    column = lax.broadcasted_iota(jnp.int32, (ROWS, ROWS), 1)

    def item(k, i):
        mine = mine_ref[:, i].reshape(ROWS, ROWS)
        theirs = theirs_ref[:, i].reshape(ROWS, ROWS)
        return jnp.where(flags_ref[2] == k, mine, theirs)

    def own(k):
        add = (row == column) & (flags_ref[k] == 1)
        return item(k, 0) + jnp.where(add, shift_ref[...], 0.0)

    inverse = jnp.where(flags_ref[2] == 1, inverse_ref[...], their_inverse_ref[...])
    remote = exact(inverse, item(0, 1), ((1,), (0,)))
    zero = exact(inverse, own(0), ((1,), (0,)))
    rest = own(1) - exact(remote, zero, ((0,), (0,)))
    out_ref[:, :ROWS] = zero.T
    second = inverse_factor(item(1, 1) - exact(remote, remote, ((0,), (0,))))
    out_ref[:, ROWS:] = exact(second, rest, ((1,), (0,))).T


def last_factor(flags, mine, theirs, shift, inverse, their_inverse):
    return pl.pallas_call(
        last_kernel,
        out_shape=jax.ShapeDtypeStruct((ROWS, 2 * ROWS), jnp.float32),
        in_specs=[SMEM] + [VMEM] * 5,
        out_specs=VMEM,
        compiler_params=pltpu.CompilerParams(vmem_limit_bytes=16 << 20),
        cost_estimate=pl.CostEstimate(flops=64 << 20, bytes_accessed=1 << 20, transcendentals=0),
    )(flags, mine, theirs, shift, inverse, their_inverse)


def flip(block, bit):
    return lax.ppermute(block, "par", [(i, i ^ bit) for i in range(PAR)])


def per_device(samples, shift, panel_ids):
    here = lax.axis_index("samp")
    place = lax.axis_index("par")
    role = 1 - lax.rem(place, 2)
    chip = lax.div(place, 2)
    mine = jnp.where(role == 0, panel_ids[0], panel_ids[1])
    theirs = jnp.where(role == 0, panel_ids[1], panel_ids[0])
    axes = ("samp", "par")

    pieces = lax.all_to_all(cut(samples), "samp", 0, 0, tiled=True)

    square = lax.dot_general(
        samples, samples, (((1,), (1,)), ((), ())), preferred_element_type=jnp.float32
    )
    for bit in (1, 16, 2, 4, 8):
        square = square + flip(square, bit)
    square = square + jnp.eye(ROWS, dtype=jnp.float32) * shift[:, None]
    strip = lax.dynamic_slice_in_dim(square, chip * TILE, TILE, 0)
    flags = jnp.stack([
        (panel_ids[0] == here).astype(jnp.int32), (panel_ids[1] == here).astype(jnp.int32), role
    ])
    pieces, strip, flags, mine, theirs = lax.optimization_barrier((pieces, strip, flags, mine[None], theirs[None]))

    sent = flip(partial_gram(theirs, pieces), 1)
    total = join(role, partial_gram(mine, pieces), sent, strip)

    total = lax.all_to_all(total, axes, 0, 0, axis_index_groups=CHIPS_THEN_SAMP, tiled=True)
    strips = total[:, SAMP]
    total = total[:, :SAMP].sum(0)

    def pick(array, k):
        return lax.dynamic_index_in_dim(array, panel_ids[k], 0, keepdims=False)

    second = jnp.where(role == 0, pick(total, 1), pick(strips, 0))
    diagonal = pick(strips, 1)
    total = jnp.stack([total, jnp.broadcast_to(second, total.shape)], 1)
    total = lax.all_to_all(total, axes, 0, 0, axis_index_groups=SAMP_THEN_CHIPS, tiled=True)
    block = total[:, 1]
    total = total.sum(0)
    total = jnp.stack([total[0], jnp.where(role == 0, total[1], diagonal)])

    copies = jnp.broadcast_to(total[None], (CHIPS,) + total.shape)
    gathered = lax.all_to_all(copies, "par", 0, 0, axis_index_groups=CHIPS_BY_CORE, tiled=True)
    inverse = first_factor(role, block)
    their_inverse = flip(inverse, 1)
    gathered, inverse, their_inverse = lax.optimization_barrier((gathered, inverse, their_inverse))
    return last_factor(flags, gathered, flip(gathered, 1), shift[None, :], inverse, their_inverse)


def solution(mesh):
    placed = (P("samp", "par"), P("samp"), P())
    return jax.shard_map(
        per_device, mesh=mesh, in_specs=placed, out_specs=P("samp", None), check_vma=False
    )
```

```python
import jax
import jax.numpy as jnp
from jax import lax
from jax.experimental import pallas as pl
from jax.experimental.pallas import tpu as pltpu
from jax.sharding import PartitionSpec as P

ROWS = 128
SAMP = 16
PAR = 32
CHIPS = PAR // 2
TILE = 8
TILES = ROWS // TILE
HIGHEST = lax.Precision.HIGHEST

OVER_CHIPS = [[[s * PAR + 2 * x + c for x in range(CHIPS)] for s in range(SAMP)] for c in range(2)]
OVER_SAMP = [[[s * PAR + 2 * x + c for s in range(SAMP)] for x in range(CHIPS)] for c in range(2)]
CHIPS_THEN_SAMP = OVER_CHIPS[1] + OVER_SAMP[0]
SAMP_THEN_CHIPS = OVER_SAMP[1] + OVER_CHIPS[0]
CHIPS_BY_CORE = [[2 * x + c for x in range(CHIPS)] for c in range(2)]


def exact(left, right, contract):
    return lax.dot_general(
        left, right, (contract, ((), ())),
        precision=HIGHEST, preferred_element_type=jnp.float32,
    )


def inverse_factor(matrix):
    lane = lax.broadcasted_iota(jnp.int32, (TILE, ROWS), 1)
    sub = lax.broadcasted_iota(jnp.int32, (TILE, ROWS), 0)
    lanes = lane[:1]
    tiles = [matrix[t * TILE:(t + 1) * TILE] for t in range(TILES)]
    for at in range(TILES):
        base = at * TILE
        rows = [tiles[at][r:r + 1] for r in range(TILE)]
        pivot = [
            [jnp.broadcast_to(rows[r][:, base + c:base + c + 1], (1, ROWS)) if c >= r else None for c in range(TILE)]
            for r in range(TILE)
        ]
        inside = (lane >= base) & (lane < base + TILE)
        near = at + 1 < TILES
        if near:
            after = jnp.where(inside, 0.0, tiles[at + 1])
            columns = [
                jnp.broadcast_to(tiles[at + 1][:, base + k:base + k + 1], (TILE, ROWS)) for k in range(TILE)
            ]
        inverse = [None] * TILE
        for k in range(TILE):
            inverse[k] = 1.0 / pivot[k][k]
            scaled = jnp.where(lanes == base + k, 1.0, rows[k])
            factors = [None] * TILE
            for i in range(k + 1, TILE):
                factors[i] = pivot[k][i] * inverse[k]
                for c in range(i, TILE):
                    pivot[i][c] = pivot[i][c] - factors[i] * pivot[k][c]
                rows[i] = jnp.where(lanes == base + k, 0.0, rows[i]) - factors[i] * scaled
            if near:
                lower = jnp.where((lanes > base + k) & (lanes < base + TILE), 0.0, scaled) * inverse[k]
                after = after - columns[k] * lower
                for i in range(k + 1, TILE):
                    columns[i] = columns[i] - factors[i] * columns[k]
        if at + 2 < TILES:
            solved = [None] * TILE
            for k in reversed(range(TILE)):
                value = jnp.where(lanes == base + k, 1.0, rows[k])
                value = jnp.where((lanes > base + k) & (lanes < base + TILE), 0.0, value)
                for c in range(TILE - 1, k, -1):
                    value = value - pivot[k][c] * solved[c]
                solved[k] = value * inverse[k]
            wide = [jnp.broadcast_to(row, (TILE, ROWS)) for row in solved]
        for t in range(at + 2, TILES):
            value = jnp.where(inside, 0.0, tiles[t])
            for k in reversed(range(TILE)):
                value = value - tiles[t][:, base + k:base + k + 1] * wide[k]
            tiles[t] = value
        if near:
            tiles[at + 1] = after
        done = None
        for r in range(TILE):
            row = jnp.where(lanes < base + r, rows[r], jnp.where(lanes == base + r, 1.0, 0.0))
            row = jnp.broadcast_to(row * lax.rsqrt(pivot[r][r]), (TILE, ROWS))
            done = row if done is None else jnp.where(sub == r, row, done)
        tiles[at] = done
    return jnp.concatenate(tiles, 0)


def cut_kernel(samples_ref, pieces_ref, held, arrived, left):
    width = pieces_ref.shape[2]
    into = [
        pltpu.make_async_copy(samples_ref.at[:, s * width:(s + 1) * width], held.at[s], arrived.at[s])
        for s in range(SAMP)
    ]
    out = [pltpu.make_async_copy(held.at[s], pieces_ref.at[s], left.at[s]) for s in range(SAMP)]
    for copy in into:
        copy.start()
    for s in range(SAMP):
        into[s].wait()
        out[s].start()
    for copy in out:
        copy.wait()


def cut(samples):
    shape = (SAMP, ROWS, samples.shape[1] // SAMP)
    return pl.pallas_call(
        cut_kernel,
        out_shape=jax.ShapeDtypeStruct(shape, samples.dtype),
        in_specs=[pl.BlockSpec(memory_space=pl.ANY)],
        out_specs=pl.BlockSpec(memory_space=pl.ANY),
        scratch_shapes=[
            pltpu.VMEM(shape, samples.dtype),
            pltpu.SemaphoreType.DMA((SAMP,)),
            pltpu.SemaphoreType.DMA((SAMP,)),
        ],
        cost_estimate=pl.CostEstimate(flops=0, bytes_accessed=4 << 20, transcendentals=0),
    )(samples)


def gram_kernel(panel_ref, pieces_ref, total_ref):
    panel = pieces_ref[panel_ref[0]]
    for block in range(SAMP):
        total_ref[:, block] = lax.dot_general(
            panel, pieces_ref[block], (((1,), (1,)), ((), ())), preferred_element_type=jnp.float32
        ).reshape(TILES, TILE, ROWS)


VMEM = pl.BlockSpec(memory_space=pltpu.VMEM)
SMEM = pl.BlockSpec(memory_space=pltpu.SMEM)


def partial_gram(panel, pieces):
    return pl.pallas_call(
        gram_kernel,
        out_shape=jax.ShapeDtypeStruct((TILES, SAMP, TILE, ROWS), jnp.float32),
        in_specs=[SMEM, VMEM],
        out_specs=VMEM,
        compiler_params=pltpu.CompilerParams(vmem_limit_bytes=16 << 20),
        cost_estimate=pl.CostEstimate(flops=1 << 28, bytes_accessed=4 << 20, transcendentals=0),
    )(panel, pieces)


def join_kernel(role_ref, mine_ref, theirs_ref, strip_ref, out_ref, held, left):
    def departure(tile, role):
        place = out_ref.at[tile, pl.ds(0, SAMP)] if role == 0 else out_ref.at[:, tile]
        return pltpu.make_async_copy(held.at[tile], place, left.at[tile])

    def strips():
        return pltpu.make_async_copy(held.at[TILES], out_ref.at[:, SAMP], left.at[TILES])

    def send(role):
        @pl.when(role_ref[0] == role)
        def _():
            for tile in range(TILES):
                held[tile] = mine_ref[tile] + theirs_ref[tile]
                departure(tile, role).start()
            for tile in range(TILES):
                departure(tile, role).wait()

    held[TILES] = jnp.broadcast_to(strip_ref[...][None], (SAMP, TILE, ROWS))
    strips().start()
    send(0)
    send(1)
    strips().wait()


def join(role, mine, theirs, strip):
    return pl.pallas_call(
        join_kernel,
        out_shape=jax.ShapeDtypeStruct((TILES, SAMP + 1, TILE, ROWS), jnp.float32),
        in_specs=[SMEM, VMEM, VMEM, VMEM],
        out_specs=pl.BlockSpec(memory_space=pl.ANY),
        scratch_shapes=[
            pltpu.VMEM((TILES + 1, SAMP, TILE, ROWS), jnp.float32),
            pltpu.SemaphoreType.DMA((TILES + 1,)),
        ],
        compiler_params=pltpu.CompilerParams(vmem_limit_bytes=16 << 20),
        cost_estimate=pl.CostEstimate(flops=1 << 20, bytes_accessed=4 << 20, transcendentals=0),
    )(role[None], mine, theirs, strip)


def first_kernel(role_ref, block_ref, inverse_ref):
    @pl.when(role_ref[0] == 0)
    def _():
        inverse_ref[...] = jnp.zeros_like(inverse_ref)

    @pl.when(role_ref[0] == 1)
    def _():
        inverse_ref[...] = inverse_factor(block_ref[...].reshape(ROWS, ROWS))


def first_factor(role, block):
    return pl.pallas_call(
        first_kernel,
        out_shape=jax.ShapeDtypeStruct((ROWS, ROWS), jnp.float32),
        in_specs=[SMEM, VMEM],
        out_specs=VMEM,
        compiler_params=pltpu.CompilerParams(vmem_limit_bytes=16 << 20),
        cost_estimate=pl.CostEstimate(flops=20 << 20, bytes_accessed=1 << 20, transcendentals=0),
    )(role[None], block)


def last_kernel(flags_ref, mine_ref, theirs_ref, shift_ref, inverse_ref, their_inverse_ref, out_ref):
    row = lax.broadcasted_iota(jnp.int32, (ROWS, ROWS), 0)
    column = lax.broadcasted_iota(jnp.int32, (ROWS, ROWS), 1)

    def item(k, i):
        mine = mine_ref[:, i].reshape(ROWS, ROWS)
        theirs = theirs_ref[:, i].reshape(ROWS, ROWS)
        return jnp.where(flags_ref[2] == k, mine, theirs)

    def own(k):
        add = (row == column) & (flags_ref[k] == 1)
        return item(k, 0) + jnp.where(add, shift_ref[...], 0.0)

    inverse = jnp.where(flags_ref[2] == 1, inverse_ref[...], their_inverse_ref[...])
    remote = exact(inverse, item(0, 1), ((1,), (0,)))
    zero = exact(inverse, own(0), ((1,), (0,)))
    rest = own(1) - exact(remote, zero, ((0,), (0,)))
    out_ref[:, :ROWS] = zero.T
    second = inverse_factor(item(1, 1) - exact(remote, remote, ((0,), (0,))))
    out_ref[:, ROWS:] = exact(second, rest, ((1,), (0,))).T


def last_factor(flags, mine, theirs, shift, inverse, their_inverse):
    return pl.pallas_call(
        last_kernel,
        out_shape=jax.ShapeDtypeStruct((ROWS, 2 * ROWS), jnp.float32),
        in_specs=[SMEM] + [VMEM] * 5,
        out_specs=VMEM,
        compiler_params=pltpu.CompilerParams(vmem_limit_bytes=16 << 20),
        cost_estimate=pl.CostEstimate(flops=64 << 20, bytes_accessed=1 << 20, transcendentals=0),
    )(flags, mine, theirs, shift, inverse, their_inverse)


def flip(block, bit):
    return lax.ppermute(block, "par", [(i, i ^ bit) for i in range(PAR)])


def per_device(samples, shift, panel_ids):
    here = lax.axis_index("samp")
    place = lax.axis_index("par")
    role = 1 - lax.rem(place, 2)
    chip = lax.div(place, 2)
    mine = jnp.where(role == 0, panel_ids[0], panel_ids[1])
    theirs = jnp.where(role == 0, panel_ids[1], panel_ids[0])
    axes = ("samp", "par")

    pieces = lax.all_to_all(cut(samples), "samp", 0, 0, tiled=True)

    square = lax.dot_general(
        samples, samples, (((1,), (1,)), ((), ())), preferred_element_type=jnp.float32
    )
    for bit in (1, 16, 2, 6, 14):
        square = square + flip(square, bit)
    square = square + jnp.eye(ROWS, dtype=jnp.float32) * shift[:, None]
    strip = lax.dynamic_slice_in_dim(square, chip * TILE, TILE, 0)
    flags = jnp.stack([
        (panel_ids[0] == here).astype(jnp.int32), (panel_ids[1] == here).astype(jnp.int32), role
    ])
    pieces, strip, flags, mine, theirs = lax.optimization_barrier((pieces, strip, flags, mine[None], theirs[None]))

    sent = flip(partial_gram(theirs, pieces), 1)
    total = join(role, partial_gram(mine, pieces), sent, strip)

    total = lax.all_to_all(total, axes, 0, 0, axis_index_groups=CHIPS_THEN_SAMP, tiled=True)
    strips = total[:, SAMP]
    total = total[:, :SAMP].sum(0)

    def pick(array, k):
        return lax.dynamic_index_in_dim(array, panel_ids[k], 0, keepdims=False)

    second = jnp.where(role == 0, pick(total, 1), pick(strips, 0))
    diagonal = pick(strips, 1)
    total = jnp.stack([total, jnp.broadcast_to(second, total.shape)], 1)
    total = lax.all_to_all(total, axes, 0, 0, axis_index_groups=SAMP_THEN_CHIPS, tiled=True)
    block = total[:, 1]
    total = total.sum(0)
    total = jnp.stack([total[0], jnp.where(role == 0, total[1], diagonal)])

    copies = jnp.broadcast_to(total[None], (CHIPS,) + total.shape)
    gathered = lax.all_to_all(copies, "par", 0, 0, axis_index_groups=CHIPS_BY_CORE, tiled=True)
    inverse = first_factor(role, block)
    their_inverse = flip(inverse, 1)
    gathered, inverse, their_inverse = lax.optimization_barrier((gathered, inverse, their_inverse))
    return last_factor(flags, gathered, flip(gathered, 1), shift[None, :], inverse, their_inverse)


def solution(mesh):
    placed = (P("samp", "par"), P("samp"), P())
    return jax.shard_map(
        per_device, mesh=mesh, in_specs=placed, out_specs=P("samp", None), check_vma=False
    )
```
